32 devices in a mesh: dp: 16 (over z, y, x), tensor: 2 (over core).
Axes of the slice: x: 2, y: 2, z: 4, core: 2. Of those that a mesh axis runs over, the one named last changes fastest.
Arguments:
- tokens: bfloat16 [32768, 768], P(('dp', 'tensor')), may hold values from -6 to 6
- query_key_value_weight: bfloat16 [3, 768, 768], P(None, None, 'tensor'), may hold values from -0.21875 to 0.21875
- output_matrix: bfloat16 [768, 768], P('tensor'), may hold values from -0.875 to 0.875
- up_matrix: bfloat16 [768, 3072], P(None, 'tensor'), may hold values from -0.21875 to 0.21875
- down_matrix: bfloat16 [3072, 768], P('tensor'), may hold values from -0.109375 to 0.109375
- adapter_down_maps: bfloat16 [768, 16], replicated, may hold values from -0.21875 to 0.21875
- adapter_up_maps: bfloat16 [2, 8, 768], P(None, None, 'tensor'), may hold values from -1 to 1
- layer_norm_gains: float32 [2, 768], replicated, may hold values from 0.25 to 1.75
- layer_norm_bias: float32 [2, 768], replicated, may hold values from -3 to 3
- cotangent: bfloat16 [32768, 768], P(('dp', 'tensor')), may hold values from -6 to 6
- maskable_positions: int32 [64, 128], P(('dp', 'tensor')), may hold values from 0 to 511, as said below
- masked_count_per_item: int32 [64], P(('dp', 'tensor')), may hold values from 32 to 128, as said below
Outputs:
- mixed: bfloat16 [32768, 768], P(('dp', 'tensor'))
- token_gradient: float32 [32768, 768], P(('dp', 'tensor'))
- adapter_up_gradients: float32 [12, 1024], P('tensor', 'dp')
The draws below stay inside these ranges and needn't reach their ends.
Inputs may be any that keep to these rules, and one draw needn't show every extreme that they name: `maskable_positions`: the 128 positions of an item are distinct; only an item's first masked_count_per_item slots are masked. `masked_count_per_item`: some item has exactly 128 masked positions and some exactly 32.
All inputs are finite; a program needn't handle non-finite values.
Results may differ from the reference program's by a relative error of at most 0.013.
The reference program's roundings to bfloat16 on the way count: a program that leaves them out, or rounds other values in their place, can miss the bound.
Values may be sent and summed in bfloat16 or wider, within the bound.
A program may use at most 128 MiB of HBM per device.

```python
import jax
import jax.numpy as jnp
from jax import lax

MODEL_WIDTH = 768
ATTENTION_HEADS = 12
HEAD_SIZE = 64
FF = 3072
ADAPTER_RANK = 8
SEQ = 512
SLOTS = 128
ITEMS = 64
TOKEN_TOTAL = 32768
N_DP = 16


def draw_maskable_positions(key, part):
    key = jax.random.fold_in(key, 11)
    item_keys = jax.random.split(key, ITEMS)
    return jax.vmap(lambda item_key: jax.random.permutation(item_key, SEQ)[:SLOTS])(item_keys).astype(jnp.int32)


def draw_masked_count_per_item(key, part):
    key = jax.random.fold_in(key, 23)
    key_counts, key_top, key_low = jax.random.split(key, 3)
    counts = jax.random.randint(key_counts, (ITEMS,), SLOTS // 4, SLOTS + 1)
    top_item = jax.random.randint(key_top, (), 0, ITEMS)
    low_item = (top_item + 1 + jax.random.randint(key_low, (), 0, ITEMS - 1)) % ITEMS
    counts = counts.at[top_item].set(SLOTS).at[low_item].set(SLOTS // 4)
    return counts.astype(jnp.int32)


def block_scale(stream_key, shape, cuts, smallest, top_value):
    factor_of, own = 1.0, jax.random.fold_in(stream_key, 6)
    for axis_at, parts in cuts:
        heights = jnp.exp(jax.random.uniform(jax.random.fold_in(own, axis_at), (parts,), jnp.float32, smallest / len(cuts), top_value / len(cuts)))
        factor_of = factor_of * jnp.repeat(heights, shape[axis_at] // parts).reshape([-1 if axis == axis_at else 1 for axis in range(len(shape))])
    return factor_of


def centred(stream_key, shape, width, bound, cuts=(), kind=jnp.bfloat16):
    loudness = block_scale(stream_key, shape, cuts, -0.22, 0.18) if cuts else 1.0
    array = jax.random.normal(stream_key, shape, jnp.float32) * width * loudness
    return jnp.minimum(jnp.maximum(array, -bound), bound).astype(kind)


def setup_inputs(seed: int = 0) -> dict:
    key_of = jax.random.split(jax.random.key(seed), 13)
    tokens = centred(key_of[0], (TOKEN_TOTAL, MODEL_WIDTH), 1.0, 6.0, ((0, 32),))
    query_key_value_weight = centred(key_of[1], (3, MODEL_WIDTH, MODEL_WIDTH), MODEL_WIDTH ** -0.5, 0.21875, ((2, 2),))
    output_matrix = centred(key_of[2], (MODEL_WIDTH, MODEL_WIDTH), (MODEL_WIDTH // 16) ** -0.5, 0.875, ((0, 2),))
    up_matrix = centred(key_of[3], (MODEL_WIDTH, FF), MODEL_WIDTH ** -0.5, 0.21875, ((1, 2),))
    down_matrix = centred(key_of[4], (FF, MODEL_WIDTH), FF ** -0.5, 0.109375, ((0, 2),))
    adapter_down_maps = centred(key_of[5], (MODEL_WIDTH, 2 * ADAPTER_RANK), MODEL_WIDTH ** -0.5, 0.21875)
    adapter_up_maps = centred(key_of[6], (2, ADAPTER_RANK, MODEL_WIDTH), (4 * ADAPTER_RANK) ** -0.5, 1.0, ((2, 2),))
    layer_norm_gains = jnp.clip(1.0 + 0.15 * jax.random.normal(key_of[7], (2, MODEL_WIDTH), jnp.float32), 0.25, 1.75)
    layer_norm_bias = centred(key_of[8], (2, MODEL_WIDTH), 0.5, 3.0, (), jnp.float32)
    cotangent = centred(key_of[9], (TOKEN_TOTAL, MODEL_WIDTH), 1.0, 6.0, ((0, 32),))
    maskable_positions = draw_maskable_positions(jax.random.fold_in(key_of[12], 71), 0)
    masked_count_per_item = draw_masked_count_per_item(jax.random.fold_in(key_of[12], 71), 0)
    return dict(tokens=tokens, query_key_value_weight=query_key_value_weight, output_matrix=output_matrix, up_matrix=up_matrix, down_matrix=down_matrix, adapter_down_maps=adapter_down_maps, adapter_up_maps=adapter_up_maps, layer_norm_gains=layer_norm_gains, layer_norm_bias=layer_norm_bias, cotangent=cotangent, maskable_positions=maskable_positions, masked_count_per_item=masked_count_per_item)


@jax.custom_vjp
def lowered_precision(v):
    return lax.optimization_barrier(v.astype(jnp.bfloat16)).astype(jnp.float32)

@jax.custom_vjp
def low_back(v):
    return v

def low_keep(v):
    return (lowered_precision(v), None)

def low_pass(kept, grad):
    return (grad,)

def back_keep(v):
    return (v, None)

def back_low(kept, grad):
    return (lowered_precision(grad),)
lowered_precision.defvjp(low_keep, low_pass)
low_back.defvjp(back_keep, back_low)

def product_highest(left, right):
    return jnp.dot(left, right, precision=lax.Precision.HIGHEST)

def layer_norm(values, weights, shift_vec):
    centre = values - lax.optimization_barrier(jnp.mean(values, axis=-1, keepdims=True))
    spread = lax.optimization_barrier(jnp.mean(centre * centre, axis=-1, keepdims=True))
    return centre * lax.rsqrt(spread + 1e-05) * weights + shift_vec

def masked_rows(positions, counts):
    slot_ids = jnp.arange(positions.shape[1], dtype=jnp.int32)
    live = slot_ids[None, :] < counts[:, None]
    places = jnp.arange(SEQ, dtype=jnp.int32)
    hits = (positions[:, :, None] == places[None, None, :]) & live[:, :, None]
    return jnp.any(hits, axis=1).astype(jnp.float32).reshape(-1)

def attend_item(triple):
    query_matrix_rows, key_matrix_rows, value_matrix_rows = triple
    scores = jnp.einsum('qhe,khe->hqk', query_matrix_rows, key_matrix_rows, precision=lax.Precision.HIGHEST)
    scores = low_back(scores * HEAD_SIZE ** (-0.5))
    attn_probs = lowered_precision(jax.nn.softmax(scores, axis=-1))
    context = jnp.einsum('hqk,khe->qhe', attn_probs, value_matrix_rows, precision=lax.Precision.HIGHEST)
    return lowered_precision(low_back(context))

def forward_pass(token_single_float, adapter_up_list, frozen_params):
    query_key_value_full, output_projected, up_projected, down_projected, adapter_down_rows, norm_gain_pair, norm_bias_pair = frozen_params
    row_count = token_single_float.shape[0]
    shape_four = (row_count // SEQ, SEQ, ATTENTION_HEADS, HEAD_SIZE)
    reduced_rows = lowered_precision(product_highest(token_single_float, adapter_down_rows))
    query_matrix_rows = product_highest(token_single_float, query_key_value_full[0]) + 2.0 * product_highest(reduced_rows[:, :ADAPTER_RANK], adapter_up_list[0])
    key_matrix_rows = product_highest(token_single_float, query_key_value_full[1])
    value_matrix_rows = product_highest(token_single_float, query_key_value_full[2]) + 2.0 * product_highest(reduced_rows[:, ADAPTER_RANK:], adapter_up_list[1])
    query_matrix_rows = lowered_precision(low_back(query_matrix_rows)).reshape(shape_four)
    key_matrix_rows = lowered_precision(low_back(key_matrix_rows)).reshape(shape_four)
    value_matrix_rows = lowered_precision(low_back(value_matrix_rows)).reshape(shape_four)
    context = lax.map(jax.checkpoint(attend_item), (query_matrix_rows, key_matrix_rows, value_matrix_rows))
    context = context.reshape(row_count, MODEL_WIDTH)
    attn_out = low_back(product_highest(context, output_projected))
    hidden = layer_norm(token_single_float + attn_out, norm_gain_pair[0], norm_bias_pair[0])
    ffn_in = low_back(product_highest(lowered_precision(hidden), up_projected))
    activated = lowered_precision(jax.nn.gelu(ffn_in, approximate=False))
    branch = low_back(product_highest(activated, down_projected))
    return layer_norm(hidden + branch, norm_gain_pair[1], norm_bias_pair[1])

def reference(tokens, query_key_value_weight, output_matrix, up_matrix, down_matrix, adapter_down_maps, adapter_up_maps, layer_norm_gains, layer_norm_bias, cotangent, maskable_positions, masked_count_per_item):
    frozen_params = (query_key_value_weight.astype(jnp.float32), output_matrix.astype(jnp.float32), up_matrix.astype(jnp.float32), down_matrix.astype(jnp.float32), adapter_down_maps.astype(jnp.float32), layer_norm_gains.astype(jnp.float32), layer_norm_bias.astype(jnp.float32))
    adapter_single_float = adapter_up_maps.astype(jnp.float32)

    def head_group_step(gradient_total, pieces):
        token_matrix_rows, cotangent_rows, positions, counts = pieces
        masked_row_flags = masked_rows(positions, counts)
        layer_outputs, backward_map = jax.vjp(lambda token_single_float, adapter_up_list: forward_pass(token_single_float, adapter_up_list, frozen_params), token_matrix_rows.astype(jnp.float32), adapter_single_float)
        gradient_rows, adapter_gradient = backward_map(cotangent_rows.astype(jnp.float32) * masked_row_flags[:, None])
        return (gradient_total + adapter_gradient, (layer_outputs.astype(jnp.bfloat16), gradient_rows))

    def grouped_by_head(source):
        return source.reshape((N_DP, -1) + source.shape[1:])
    gradient_total, (mixed, token_gradient) = lax.scan(head_group_step, jnp.zeros(adapter_single_float.shape, jnp.float32), (grouped_by_head(tokens), grouped_by_head(cotangent), grouped_by_head(maskable_positions), grouped_by_head(masked_count_per_item)))
    adapter_up_gradients = gradient_total.reshape(2, ADAPTER_RANK, ATTENTION_HEADS, HEAD_SIZE).transpose(2, 0, 1, 3).reshape(ATTENTION_HEADS, 2 * ADAPTER_RANK * HEAD_SIZE)
    return (mixed.reshape(TOKEN_TOTAL, MODEL_WIDTH), token_gradient.reshape(TOKEN_TOTAL, MODEL_WIDTH), adapter_up_gradients)
```

```python
import functools

import jax
import jax.numpy as jnp
import numpy as np
from jax import lax
from jax.experimental import pallas as pl
from jax.experimental.pallas import tpu as pltpu
from jax.sharding import PartitionSpec as P

HEAD_SIZE = 64
ADAPTER_RANK = 8
SEQ = 512
PAIR = 2 * HEAD_SIZE
NORM_EPS = 1e-05
ROOT_HALF = np.float32(0.5**0.5)
GAUSS = np.float32(1.0 / np.sqrt(2.0 * np.pi))
MESH = pl.DeviceIdType.MESH
bf16 = jnp.bfloat16
f32 = jnp.float32


def mm(left, right):
    return jnp.dot(left, right, preferred_element_type=f32)


def mm_t(left, right):
    return lax.dot_general(left, right, (((1,), (1,)), ((), ())), preferred_element_type=f32)


def t_mm(left, right):
    return lax.dot_general(left, right, (((0,), (0,)), ((), ())), preferred_element_type=f32)


def norm(values):
    centre = values - jnp.mean(values, axis=-1, keepdims=True)
    inverse = lax.rsqrt(jnp.mean(centre * centre, axis=-1, keepdims=True) + NORM_EPS)
    return centre * inverse, inverse


def norm_back(scaled, normed, inverse):
    centred = scaled - jnp.mean(scaled, axis=-1, keepdims=True)
    return inverse * (centred - normed * jnp.mean(scaled * normed, axis=-1, keepdims=True))


def gelu_cdf(v):
    return 0.5 + 0.5 * lax.erf(v * ROOT_HALF)


def gelu_slope(v):
    return gelu_cdf(v) + v * (GAUSS * jnp.exp(-0.5 * v * v))


def layer_kernel(
    n_dp,
    items,
    slots,
    width,
    ff,
    tokens_hbm,
    qkv_hbm,
    o_hbm,
    up_hbm,
    down_hbm,
    a_ref,
    b_hbm,
    gain_ref,
    bias_ref,
    cot_hbm,
    pos_ref,
    count_ref,
    mixed_hbm,
    tg_hbm,
    adapter_ref,
    x,
    xp,
    wq,
    wkv,
    wo,
    wup,
    wdown,
    bmat,
    cot,
    mt,
    red_q,
    red_v,
    kv,
    q8,
    ctx,
    probs,
    hid,
    normed_one,
    normed_two,
    inverses,
    ffn_in,
    mixed_p,
    gq,
    gkv,
    grad_one,
    tg,
    part_out,
    part_in,
    send_block,
    recv_block,
    load_sem,
    send_sem,
    recv_sem,
    out_sem,
    part_sem,
    peer_send_sem,
    peer_recv_sem,
):
    half = width // 2
    half_ff = ff // 2
    pairs_half = half // PAIR
    rest = SEQ - slots
    n_masked = items * slots
    me = lax.axis_index("dp")
    core = lax.axis_index("tensor")
    sibling = {"tensor": 1 - core}

    barrier = pltpu.get_barrier_semaphore()
    pl.semaphore_signal(barrier, inc=1, device_id=sibling, device_id_type=MESH)

    def greet(j, c):
        peer = lax.rem(me + j, n_dp)
        pl.semaphore_signal(barrier, inc=1, device_id={"dp": peer}, device_id_type=MESH)
        return c

    lax.fori_loop(1, n_dp, greet, 0)

    loads = {}

    def load(name, src, dst):
        loads[name] = pltpu.make_async_copy(src, dst, load_sem.at[len(loads)])
        loads[name].start()

    load("x", tokens_hbm, x)
    load("k", qkv_hbm.at[1], wkv.at[0, :, pl.ds(0, half)])
    load("v", qkv_hbm.at[2], wkv.at[0, :, pl.ds(half, half)])
    load("b", b_hbm, bmat.at[0])
    load("q", qkv_hbm.at[0], wq.at[:, pl.ds(0, half)])
    load("o", o_hbm, wo.at[pl.ds(0, half)])
    load("up", up_hbm, wup.at[:, pl.ds(0, half_ff)])
    load("down", down_hbm, wdown.at[pl.ds(0, half_ff)])
    load("cot", cot_hbm, cot)

    for i in range(items):
        place = lax.broadcasted_iota(jnp.int32, (SEQ, slots), 0)
        slot_pos = pos_ref[pl.ds(i, 1), :]
        hit = slot_pos == place
        before = jnp.sum((slot_pos < place).astype(f32), axis=1, keepdims=True)
        taken = jnp.sum(hit.astype(f32), axis=1, keepdims=True)
        own_place = lax.broadcasted_iota(jnp.int32, (SEQ, 1), 0).astype(f32)
        rank = jnp.where(taken > 0.5, -1.0, own_place - before)
        column = lax.broadcasted_iota(jnp.int32, (SEQ, rest), 1).astype(f32)
        mt[i, :, pl.ds(0, slots)] = hit.astype(f32).astype(bf16)
        mt[i, :, pl.ds(slots, rest)] = (rank == column).astype(f32).astype(bf16)

    pl.semaphore_wait(barrier, n_dp)

    gets = {}

    def send(name, src, dst):
        n = len(gets)
        gets[name] = pltpu.make_async_remote_copy(
            src_ref=src,
            dst_ref=dst,
            send_sem=send_sem.at[n],
            recv_sem=recv_sem.at[n],
            device_id=sibling,
            device_id_type=MESH,
        )
        gets[name].start()

    send("b", b_hbm, bmat.at[1])
    send("q", qkv_hbm.at[0], wq.at[:, pl.ds(half, half)])
    send("k", qkv_hbm.at[1], wkv.at[1, :, pl.ds(0, half)])
    send("v", qkv_hbm.at[2], wkv.at[1, :, pl.ds(half, half)])
    send("o", o_hbm, wo.at[pl.ds(half, half)])
    send("up", up_hbm, wup.at[:, pl.ds(half_ff, half_ff)])
    send("down", down_hbm, wdown.at[pl.ds(half_ff, half_ff)])

    def rows_of(i):
        return (
            (0, slots, pl.ds(i * slots, slots)),
            (slots, rest, pl.ds(n_masked + i * rest, rest)),
        )

    lane = lax.broadcasted_iota(jnp.int32, (SEQ, 2 * ADAPTER_RANK), 1)
    loads["x"].wait()
    for i in range(items):
        item_rows = pl.ds(i * SEQ, SEQ)
        xi = x[item_rows, :]
        reduced = mm(xi, a_ref[...]).astype(bf16)
        doubled = reduced * 2
        red_v[item_rows, :] = jnp.where(lane >= ADAPTER_RANK, doubled, jnp.zeros_like(doubled))
        ordered_red = t_mm(mt[i], jnp.where(lane < ADAPTER_RANK, doubled, jnp.zeros_like(doubled)))
        ordered = t_mm(mt[i], xi)
        for start, size, rows in rows_of(i):
            xp[rows, :] = ordered[start : start + size].astype(bf16)
            red_q[rows, :] = ordered_red[start : start + size].astype(bf16)

    def stacked_b(h):
        return bmat[h].astype(f32).reshape(2 * ADAPTER_RANK, half).astype(bf16)

    def project_kv(h):
        for i in range(items):
            rows = pl.ds(i * SEQ, SEQ)
            out = mm(x[rows, :], wkv[h])
            kv[h, rows, pl.ds(0, half)] = out[:, :half].astype(bf16)
            kv[h, rows, pl.ds(half, half)] = (
                out[:, half:] + mm(red_v[rows, :], stacked_b(h))
            ).astype(bf16)

    loads["k"].wait()
    loads["v"].wait()
    loads["b"].wait()
    project_kv(0)

    loads["q"].wait()
    gets["b"].wait()
    gets["q"].wait()
    both_b = jnp.concatenate([stacked_b(0), stacked_b(1)], axis=1)
    out = mm(xp[...], wq[...]) + mm(red_q[...], both_b)
    q8[...] = out.astype(bf16) * np.float32(HEAD_SIZE**-0.5).astype(bf16)

    def halves(block):
        low = lax.broadcasted_iota(jnp.int32, block.shape, 1) < HEAD_SIZE
        zero = jnp.zeros_like(block)
        return jnp.concatenate([jnp.where(low, block, zero), jnp.where(low, zero, block)], axis=0)

    def joined(both):
        n = both.shape[0] // 2
        low = lax.broadcasted_iota(jnp.int32, (n, PAIR), 1) < HEAD_SIZE
        return jnp.where(low, both[:n], both[n:])

    def attend(i, h, c):
        columns = pl.ds((h * pairs_half + c) * PAIR, PAIR)
        item_rows = pl.ds(i * SEQ, SEQ)
        keys = kv[h, item_rows, pl.ds(c * PAIR, PAIR)]
        values = kv[h, item_rows, pl.ds(half + c * PAIR, PAIR)]
        wide = jnp.concatenate([values, jnp.ones_like(values)], axis=1)
        starts = [i * slots] + [n_masked + i * rest + r for r in range(0, rest, 128)]
        for n, start in enumerate(starts):
            rows = pl.ds(start, 128)
            scores = mm_t(halves(q8[rows, columns]), keys)
            expo = jnp.exp(scores - jnp.max(scores, axis=-1, keepdims=True))
            both = mm(expo.astype(bf16), wide)
            share = 1.0 / both[:, PAIR:]
            ctx[rows, columns] = joined(both[:, :PAIR] * share).astype(bf16)
            if n == 0:
                probs[(i * 2 + h) * pairs_half + c] = expo * share[:, :1]

    for i in range(items):
        for c in range(pairs_half):
            attend(i, 0, c)
    gets["k"].wait()
    gets["v"].wait()
    project_kv(1)
    for i in range(items):
        for c in range(pairs_half):
            attend(i, 1, c)

    loads["o"].wait()
    gets["o"].wait()
    step = 256
    row_steps = [pl.ds(r, step) for r in range(0, items * SEQ, step)]
    for n, rows in enumerate(row_steps):
        normed, inverse = norm(xp[rows, :].astype(f32) + mm(ctx[rows, :], wo[...]))
        hid[rows, :] = normed * gain_ref[pl.ds(0, 1), :] + bias_ref[pl.ds(0, 1), :]
        if n == 0:
            normed_one[...] = normed
            inverses[0] = jnp.broadcast_to(inverse, inverses.shape[1:])

    loads["up"].wait()
    gets["up"].wait()
    loads["down"].wait()
    gets["down"].wait()
    piece = 1536

    def keep_mixed(first, value):
        done = 0
        while done < step:
            row = first + done
            if row < n_masked:
                i, at = divmod(row, slots)
                size = min(step - done, slots - at)
            else:
                i, at = divmod(row - n_masked, rest)
                size = min(step - done, rest - at)
                at += slots
            mixed_p[i, pl.ds(at, size), :] = value[done : done + size]
            done += size

    for n, rows in enumerate(row_steps):
        hidden = hid[rows, :]
        low = hidden.astype(bf16)
        total = hidden
        for s in range(0, ff, piece):
            inner = mm(low, wup[:, pl.ds(s, piece)])
            if n == 0:
                ffn_in[:, pl.ds(s, piece)] = inner
            total = total + mm((inner * gelu_cdf(inner)).astype(bf16), wdown[pl.ds(s, piece), :])
        normed, inverse = norm(total)
        if n == 0:
            normed_two[...] = normed
            inverses[1] = jnp.broadcast_to(inverse, inverses.shape[1:])
        keep_mixed(
            n * step,
            (normed * gain_ref[pl.ds(1, 1), :] + bias_ref[pl.ds(1, 1), :]).astype(bf16),
        )

    loads["cot"].wait()
    upstream = []
    for i in range(items):
        live = lax.broadcasted_iota(jnp.int32, (slots, 1), 0) < count_ref[i]
        picked = t_mm(mt[i, :, pl.ds(0, slots)], cot[pl.ds(i * SEQ, SEQ), :])
        upstream.append(jnp.where(live, picked, 0.0))
    grad_out = jnp.concatenate(upstream, axis=0)
    grad_two = norm_back(
        grad_out * gain_ref[pl.ds(1, 1), :], normed_two[...], inverses[1][:, :1]
    )
    grad_two_low = grad_two.astype(bf16)
    grad_hidden = grad_two
    for s in range(0, ff, piece):
        grad_inner = (
            gelu_slope(ffn_in[:, pl.ds(s, piece)]) * mm_t(grad_two_low, wdown[pl.ds(s, piece), :])
        ).astype(bf16)
        grad_hidden = grad_hidden + mm_t(grad_inner, wup[:, pl.ds(s, piece)])
    grad_one[...] = norm_back(
        grad_hidden * gain_ref[pl.ds(0, 1), :], normed_one[...], inverses[0][:, :1]
    )
    grad_context = mm_t(grad_one[...].astype(bf16), wo[...]).astype(bf16)

    eighth = np.float32(HEAD_SIZE**-0.5)

    def attend_back(i, h, c):
        pair = h * pairs_half + c
        columns = pl.ds(pair * PAIR, PAIR)
        item_rows = pl.ds(i * SEQ, SEQ)
        rows = pl.ds(i * slots, slots)
        keys = kv[h, item_rows, pl.ds(c * PAIR, PAIR)]
        values = kv[h, item_rows, pl.ds(half + c * PAIR, PAIR)]
        share = probs[(i * 2 + h) * pairs_half + c]
        grad_ctx = halves(
            grad_context[i * slots : (i + 1) * slots, pair * PAIR : (pair + 1) * PAIR]
        )
        grad_probs = mm_t(grad_ctx, values)
        inner = jnp.sum(share * grad_probs, axis=-1, keepdims=True)
        grad_scores = (share * (grad_probs - inner)).astype(bf16)
        gq[rows, columns] = (joined(mm(grad_scores, keys)) * eighth).astype(bf16)
        gkv[h, item_rows, pl.ds(c * PAIR, PAIR)] = t_mm(
            grad_scores, halves(q8[rows, columns])
        ).astype(bf16)
        gkv[h, item_rows, pl.ds(half + c * PAIR, PAIR)] = t_mm(
            share.astype(bf16), grad_ctx
        ).astype(bf16)

    for i in range(items):
        for h in range(2):
            for c in range(pairs_half):
                attend_back(i, h, c)

    q_part = t_mm(red_q[pl.ds(0, n_masked), :], gq[...])
    own_part = q_part[:, :half] + t_mm(red_v[...], gkv[0, :, pl.ds(half, half)])
    part_out[...] = q_part[:, half:] + t_mm(red_v[...], gkv[1, :, pl.ds(half, half)])
    to_sibling = pltpu.make_async_remote_copy(
        src_ref=part_out,
        dst_ref=part_in,
        send_sem=part_sem.at[0],
        recv_sem=part_sem.at[1],
        device_id=sibling,
        device_id_type=MESH,
    )
    to_sibling.start()

    for i in range(items):
        x[pl.ds(i * SEQ, SEQ), :] = mm(mt[i], mixed_p[i]).astype(bf16)
    mixed_copy = pltpu.make_async_copy(x, mixed_hbm, out_sem.at[0])
    mixed_copy.start()

    to_sibling.wait()
    summed = own_part + part_in[...]
    for r in range(2 * ADAPTER_RANK):
        for g in range(pairs_half):
            send_block[r, pl.ds(g, 1), :] = summed[r : r + 1, g * PAIR : (g + 1) * PAIR]
    block_rows = recv_block.shape[1]

    def block_of(j):
        return send_block.at[pl.ds(lax.div(j * (2 * ADAPTER_RANK), n_dp), block_rows)]

    def peer_copy(j):
        peer = lax.rem(me + j, n_dp)
        return pltpu.make_async_remote_copy(
            src_ref=block_of(peer),
            dst_ref=recv_block.at[me],
            send_sem=peer_send_sem.at[j],
            recv_sem=peer_recv_sem.at[j],
            device_id={"dp": peer},
            device_id_type=MESH,
        )

    def send_peer(j, c):
        peer_copy(j).start()
        return c

    lax.fori_loop(1, n_dp, send_peer, 0)
    own_copy = pltpu.make_async_copy(block_of(me), recv_block.at[me], part_sem.at[2])
    own_copy.start()

    a_low = a_ref[...]

    def low_rank(rows_gradient, b_rows):
        reduced_gradient = 2.0 * mm_t(rows_gradient, b_rows)
        high = reduced_gradient.astype(bf16)
        low = (reduced_gradient - high.astype(f32)).astype(bf16)
        return mm_t(high, a_low) + mm_t(low, a_low)

    row16 = lax.broadcasted_iota(jnp.int32, (2 * ADAPTER_RANK, width), 0)
    q_b = jnp.where(row16 < ADAPTER_RANK, both_b, jnp.zeros_like(both_b))
    v_b = jnp.where(row16 >= ADAPTER_RANK, both_b, jnp.zeros_like(both_b))
    compact = grad_one[...] + mm_t(gq[...], wq[...]) + low_rank(gq[...], q_b)
    high = compact.astype(bf16)
    low = (compact - high.astype(f32)).astype(bf16)
    for i in range(items):
        rows = pl.ds(i * SEQ, SEQ)
        own_rows = slice(i * slots, (i + 1) * slots)
        back = mt[i, :, pl.ds(0, slots)]
        v_gradient = jnp.concatenate(
            [gkv[0, rows, pl.ds(half, half)], gkv[1, rows, pl.ds(half, half)]], axis=1
        )
        tg[rows, :] = (
            mm_t(gkv[0, rows, :], wkv[0])
            + mm_t(gkv[1, rows, :], wkv[1])
            + low_rank(v_gradient, v_b)
            + mm(
                jnp.concatenate([back, back], axis=1),
                jnp.concatenate([high[own_rows], low[own_rows]], axis=0),
            )
        )
    tg_copy = pltpu.make_async_copy(tg, tg_hbm, out_sem.at[1])
    tg_copy.start()

    own_copy.wait()

    def wait_peer(j, c):
        peer_copy(j).wait()
        return c

    lax.fori_loop(1, n_dp, wait_peer, 0)
    adapter_ref[...] = jnp.sum(recv_block[...], axis=0)

    for name in gets:
        if name in ("x",):
            gets[name].wait()
    mixed_copy.wait()
    tg_copy.wait()


def local(
    tokens,
    query_key_value_weight,
    output_matrix,
    up_matrix,
    down_matrix,
    adapter_down_maps,
    adapter_up_maps,
    layer_norm_gains,
    layer_norm_bias,
    cotangent,
    maskable_positions,
    masked_count_per_item,
    *,
    n_dp,
):
    rows, width = tokens.shape
    items, slots = maskable_positions.shape
    ff = 2 * up_matrix.shape[1]
    half = width // 2
    n_masked = items * slots
    pairs = width // PAIR
    block_rows = max(1, 2 * ADAPTER_RANK // n_dp)
    anywhere = pl.BlockSpec(memory_space=pl.ANY)
    vmem = pl.BlockSpec(memory_space=pltpu.VMEM)
    smem = pl.BlockSpec(memory_space=pltpu.SMEM)
    mixed, token_gradient, blocks = pl.pallas_call(
        functools.partial(layer_kernel, n_dp, items, slots, width, ff),
        out_shape=(
            jax.ShapeDtypeStruct((rows, width), bf16),
            jax.ShapeDtypeStruct((rows, width), f32),
            jax.ShapeDtypeStruct((block_rows, 8, PAIR), f32),
        ),
        in_specs=[
            anywhere, anywhere, anywhere, anywhere, anywhere,
            vmem, anywhere, vmem, vmem, anywhere, vmem, smem,
        ],
        out_specs=(anywhere, anywhere, vmem),
        scratch_shapes=[
            pltpu.VMEM((rows, width), bf16),
            pltpu.VMEM((rows, width), bf16),
            pltpu.VMEM((width, width), bf16),
            pltpu.VMEM((2, width, width), bf16),
            pltpu.VMEM((width, width), bf16),
            pltpu.VMEM((width, ff), bf16),
            pltpu.VMEM((ff, width), bf16),
            pltpu.VMEM((2, 2, ADAPTER_RANK, half), bf16),
            pltpu.VMEM((rows, width), bf16),
            pltpu.VMEM((items, SEQ, SEQ), bf16),
            pltpu.VMEM((rows, 2 * ADAPTER_RANK), bf16),
            pltpu.VMEM((rows, 2 * ADAPTER_RANK), bf16),
            pltpu.VMEM((2, rows, width), bf16),
            pltpu.VMEM((rows, width), bf16),
            pltpu.VMEM((rows, width), bf16),
            pltpu.VMEM((items * pairs, 2 * slots, SEQ), f32),
            pltpu.VMEM((rows, width), f32),
            pltpu.VMEM((n_masked, width), f32),
            pltpu.VMEM((n_masked, width), f32),
            pltpu.VMEM((2, n_masked, 128), f32),
            pltpu.VMEM((n_masked, ff), f32),
            pltpu.VMEM((items, SEQ, width), bf16),
            pltpu.VMEM((n_masked, width), bf16),
            pltpu.VMEM((2, rows, width), bf16),
            pltpu.VMEM((n_masked, width), f32),
            pltpu.VMEM((rows, width), f32),
            pltpu.VMEM((2 * ADAPTER_RANK, half), f32),
            pltpu.VMEM((2 * ADAPTER_RANK, half), f32),
            pltpu.VMEM((2 * ADAPTER_RANK, 8, PAIR), f32),
            pltpu.VMEM((n_dp, block_rows, 8, PAIR), f32),
            pltpu.SemaphoreType.DMA((9,)),
            pltpu.SemaphoreType.DMA((7,)),
            pltpu.SemaphoreType.DMA((7,)),
            pltpu.SemaphoreType.DMA((2,)),
            pltpu.SemaphoreType.DMA((3,)),
            pltpu.SemaphoreType.DMA((n_dp,)),
            pltpu.SemaphoreType.DMA((n_dp,)),
        ],
        compiler_params=pltpu.CompilerParams(
            collective_id=0, has_side_effects=True, vmem_limit_bytes=62 * 2**20
        ),
    )(
        tokens,
        query_key_value_weight,
        output_matrix,
        up_matrix,
        down_matrix,
        adapter_down_maps,
        adapter_up_maps,
        layer_norm_gains,
        layer_norm_bias,
        cotangent,
        maskable_positions,
        masked_count_per_item,
    )
    heads = half // HEAD_SIZE
    by_head = blocks[:, : half // PAIR, :].reshape(block_rows, heads, HEAD_SIZE).transpose(1, 0, 2)
    by_head = by_head.reshape(heads, block_rows * HEAD_SIZE)
    share = 2 * ADAPTER_RANK * HEAD_SIZE // n_dp
    if share < HEAD_SIZE:
        at = lax.rem(lax.axis_index("dp"), HEAD_SIZE // share) * share
        by_head = lax.dynamic_slice(by_head, (0, at), (heads, share))
    return mixed, token_gradient, by_head


def solution(mesh):
    return jax.shard_map(
        functools.partial(local, n_dp=mesh.shape["dp"]),
        mesh=mesh,
        in_specs=(
            P(("dp", "tensor"), None),
            P(None, None, "tensor"),
            P("tensor", None),
            P(None, "tensor"),
            P("tensor", None),
            P(),
            P(None, None, "tensor"),
            P(),
            P(),
            P(("dp", "tensor"), None),
            P(("dp", "tensor"), None),
            P(("dp", "tensor")),
        ),
        out_specs=(P(("dp", "tensor"), None), P(("dp", "tensor"), None), P("tensor", "dp")),
        check_vma=False,
    )
```

```python
import functools

import jax
import jax.numpy as jnp
import numpy as np
from jax import lax
from jax.experimental import pallas as pl
from jax.experimental.pallas import tpu as pltpu
from jax.sharding import PartitionSpec as P

HEAD_SIZE = 64
ADAPTER_RANK = 8
RANKS = 2 * ADAPTER_RANK
SEQ = 512
PAIR = 2 * HEAD_SIZE
NORM_EPS = 1e-05
ROOT_HALF = np.float32(0.5**0.5)
GAUSS = np.float32(1.0 / np.sqrt(2.0 * np.pi))
MESH = pl.DeviceIdType.MESH
LOOPS = dict(att=False, kv=False, ffn=True, aback=False, tg=True, out=True, q=False)
bf16 = jnp.bfloat16
f32 = jnp.float32


def mm(left, right):
    return jnp.dot(left, right, preferred_element_type=f32)


def mm_t(left, right):
    return lax.dot_general(left, right, (((1,), (1,)), ((), ())), preferred_element_type=f32)


def t_mm(left, right):
    return lax.dot_general(left, right, (((0,), (0,)), ((), ())), preferred_element_type=f32)


def norm(values):
    centre = values - jnp.mean(values, axis=-1, keepdims=True)
    inverse = lax.rsqrt(jnp.mean(centre * centre, axis=-1, keepdims=True) + NORM_EPS)
    return centre * inverse, inverse


def norm_back(scaled, normed, inverse):
    centred = scaled - jnp.mean(scaled, axis=-1, keepdims=True)
    return inverse * (centred - normed * jnp.mean(scaled * normed, axis=-1, keepdims=True))


def staged(steps, *stages):
    held = [None] * len(steps)
    for t in range(len(steps) + len(stages) - 1):
        for n, stage in enumerate(stages):
            if 0 <= t - n < len(steps):
                held[t - n] = stage(steps[t - n], held[t - n])
    return held


def each(count, body, loop=True):
    if not loop:
        for n in range(count):
            body(n)
        return

    def one(n, c):
        body(n)
        return c

    lax.fori_loop(0, count, one, 0)


def rows_at(first, n, size):
    start = first + n * size
    return pl.ds(start if isinstance(start, int) else pl.multiple_of(start, 128), size)


def halves(block):
    low = lax.broadcasted_iota(jnp.int32, block.shape, 1) < HEAD_SIZE
    zero = jnp.zeros_like(block)
    return jnp.concatenate([jnp.where(low, block, zero), jnp.where(low, zero, block)], axis=0)


def halves_across(block):
    turned = block.T
    low = lax.broadcasted_iota(jnp.int32, turned.shape, 0) < HEAD_SIZE
    zero = jnp.zeros_like(turned)
    return jnp.concatenate([jnp.where(low, turned, zero), jnp.where(low, zero, turned)], axis=1)


def joined(both):
    n = both.shape[0] // 2
    low = lax.broadcasted_iota(jnp.int32, (n, PAIR), 1) < HEAD_SIZE
    return jnp.where(low, both[:n], both[n:])


def adapter_rows(both_b, first):
    is_first = lax.broadcasted_iota(jnp.int32, both_b.shape, 0) < ADAPTER_RANK
    rows = jnp.where(is_first == first, both_b, jnp.zeros_like(both_b))
    blank = jnp.zeros((128 - 2 * RANKS, both_b.shape[1]), bf16)
    return jnp.concatenate([rows, rows, blank], axis=0)


def high_and_low(twice):
    high = twice.astype(bf16)
    low = (twice - high.astype(f32)).astype(bf16)
    column = lax.broadcasted_iota(jnp.int32, twice.shape, 1)
    return jnp.where(column < RANKS, high, low)


def maps_twice(a):
    blank = jnp.zeros((128 - 2 * RANKS, a.shape[1]), bf16)
    return jnp.concatenate([a, a, blank], axis=0)


def layer_kernel(
    n_dp,
    items,
    slots,
    width,
    ff,
    tokens_hbm,
    qkv_hbm,
    o_hbm,
    up_hbm,
    down_hbm,
    a_hbm,
    b_hbm,
    gain_hbm,
    bias_hbm,
    cot_hbm,
    pos_hbm,
    count_hbm,
    mt,
    wkv_out,
    gkv,
    compact,
    mixed_p,
    both_b,
    recv_block,
    a_ref,
    gain_ref,
    bias_ref,
    pos_ref,
    count_ref,
    x,
    xp,
    wq,
    wkv,
    wo,
    wup,
    wdown,
    bmat,
    cot,
    red_q,
    red_v,
    kv,
    q8,
    ctx,
    probs,
    hid,
    normed_one,
    normed_two,
    inverses,
    slope,
    branch,
    gq,
    grad_one,
    grad_context,
    part_own,
    part_out,
    part_in,
    send_block,
    load_sem,
    send_sem,
    recv_sem,
    part_sem,
    peer_send_sem,
    peer_recv_sem,
):
    half = width // 2
    half_ff = ff // 2
    pairs_half = half // PAIR
    rest = SEQ - slots
    n_masked = items * slots
    me = lax.axis_index("dp")
    core = lax.axis_index("tensor")
    sibling = {"tensor": 1 - core}
    loads = {}
    gets = {}

    def load(name, src, dst):
        loads[name] = pltpu.make_async_copy(src, dst, load_sem.at[len(loads)])
        loads[name].start()

    def load_halves():
        load("x", tokens_hbm, x)
        load("a", a_hbm, a_ref)
        load("pos", pos_hbm, pos_ref)
        load("b", b_hbm, bmat.at[0])
        load("k", qkv_hbm.at[1], wkv.at[0, :, pl.ds(0, half)])
        load("v", qkv_hbm.at[2], wkv.at[0, :, pl.ds(half, half)])
        load("q", qkv_hbm.at[0], wq.at[:, pl.ds(0, half)])
        load("gain", gain_hbm, gain_ref)
        load("bias", bias_hbm, bias_ref)
        load("count", count_hbm, count_ref)
        load("o", o_hbm, wo.at[pl.ds(0, half)])
        load("up", up_hbm, wup.at[:, pl.ds(0, half_ff)])
        load("down", down_hbm, wdown.at[pl.ds(0, half_ff)])
        load("cot", cot_hbm, cot)

    barrier = pltpu.get_barrier_semaphore()

    def greet():
        pl.semaphore_signal(barrier, inc=1, device_id=sibling, device_id_type=MESH)

        def one(j, c):
            peer = lax.rem(me + j, n_dp)
            pl.semaphore_signal(barrier, inc=1, device_id={"dp": peer}, device_id_type=MESH)
            return c

        lax.fori_loop(1, n_dp, one, 0)

    def send(name, src, dst):
        n = len(gets)
        gets[name] = pltpu.make_async_remote_copy(
            src_ref=src,
            dst_ref=dst,
            send_sem=send_sem.at[n],
            recv_sem=recv_sem.at[n],
            device_id=sibling,
            device_id_type=MESH,
        )
        gets[name].start()

    def send_halves():
        send("b", b_hbm, bmat.at[1])
        send("k", qkv_hbm.at[1], wkv.at[1, :, pl.ds(0, half)])
        send("v", qkv_hbm.at[2], wkv.at[1, :, pl.ds(half, half)])
        send("q", qkv_hbm.at[0], wq.at[:, pl.ds(half, half)])
        send("o", o_hbm, wo.at[pl.ds(half, half)])
        send("up", up_hbm, wup.at[:, pl.ds(half_ff, half_ff)])
        send("down", down_hbm, wdown.at[pl.ds(half_ff, half_ff)])

    def wait(which, *names):
        for name in names:
            which[name].wait()

    def order(i):
        place = lax.broadcasted_iota(jnp.int32, (SEQ, slots), 0)
        slot_pos = pos_ref[pl.ds(i, 1), :]
        hit = slot_pos == place
        before = jnp.sum((slot_pos < place).astype(f32), axis=1, keepdims=True)
        taken = jnp.sum(hit.astype(f32), axis=1, keepdims=True)
        own_place = lax.broadcasted_iota(jnp.int32, (SEQ, 1), 0).astype(f32)
        rank = jnp.where(taken > 0.5, -1.0, own_place - before)
        column = lax.broadcasted_iota(jnp.int32, (SEQ, rest), 1).astype(f32)
        mt[i, :, pl.ds(0, slots)] = hit.astype(f32).astype(bf16)
        mt[i, :, pl.ds(slots, rest)] = (rank == column).astype(f32).astype(bf16)

    def rows_of(i):
        return (
            (0, slots, pl.ds(i * slots, slots)),
            (slots, rest, pl.ds(n_masked + i * rest, rest)),
        )

    lane = lax.broadcasted_iota(jnp.int32, (SEQ, RANKS), 1)

    def reduce_rows(i):
        rows = pl.ds(i * SEQ, SEQ)
        doubled = mm_t(x[rows, :], a_ref[...]).astype(bf16) * 2
        zero = jnp.zeros_like(doubled)
        red_v[rows, :] = jnp.where(lane >= ADAPTER_RANK, doubled, zero)
        return jnp.where(lane < ADAPTER_RANK, doubled, zero)

    def reorder(i, reduced):
        ordered = t_mm(mt[i], x[pl.ds(i * SEQ, SEQ), :])
        ordered_red = t_mm(mt[i], reduced)
        for start, size, rows in rows_of(i):
            xp[rows, :] = ordered[start : start + size].astype(bf16)
            red_q[rows, :] = ordered_red[start : start + size].astype(bf16)

    def stack_b(h):
        both_b[:, pl.ds(h * half, half)] = bmat[h].astype(f32).reshape(RANKS, half).astype(bf16)

    def stacked_b(h):
        return both_b[:, pl.ds(h * half, half)]

    def project_kv(h, i):
        rows = rows_at(0, i, SEQ)
        out = mm(x[rows, :], wkv[h])
        kv[h, rows, pl.ds(0, half)] = out[:, :half].astype(bf16)
        kv[h, rows, pl.ds(half, half)] = (
            out[:, half:] + mm(red_v[rows, :], stacked_b(h))
        ).astype(bf16)

    eighth = np.float32(HEAD_SIZE**-0.5)

    def project_q(h):
        columns = pl.ds(h * half, half)

        def one(i):
            rows = rows_at(0, i, SEQ)
            out = mm(xp[rows, :], wq[:, columns]) + mm(red_q[rows, :], stacked_b(h))
            q8[rows, columns] = out.astype(bf16) * eighth.astype(bf16)

        each(items, one, LOOPS["q"])

    def pair_refs(i, h, c):
        rows = rows_at(0, i, SEQ)
        return kv.at[h, rows, pl.ds(c * PAIR, PAIR)], kv.at[h, rows, pl.ds(half + c * PAIR, PAIR)]

    def attention(h):
        def where(step):
            return step[3], pl.ds((h * pairs_half + step[1]) * PAIR, PAIR)

        def score(step, _):
            return mm_t(halves(q8[where(step)]), pair_refs(step[0], h, step[1])[0][...])

        def top(step, scores):
            return scores, jnp.max(scores, axis=-1, keepdims=True)

        def power(step, held):
            return jnp.exp(held[0] - held[1])

        def mix(step, expo):
            values = pair_refs(step[0], h, step[1])[1][...]
            both = mm(expo.astype(bf16), jnp.concatenate([values, jnp.ones_like(values)], axis=1))
            share = 1.0 / both[:, PAIR:]
            ctx[where(step)] = joined(both[:, :PAIR] * share).astype(bf16)
            if step[2] == 0:
                probs[(step[0] * 2 + h) * pairs_half + step[1]] = expo * share[:, :1]

        def steps(i):
            starts = [rows_at(0, i, slots)]
            for r in range(0, rest, 128):
                start = n_masked + r + i * rest
                starts.append(pl.ds(start if isinstance(start, int) else pl.multiple_of(start, 128), 128))
            return [(i, c, n, start) for c in range(pairs_half) for n, start in enumerate(starts)]

        if LOOPS["att"]:
            each(items, lambda i: staged(steps(i), score, top, power, mix))
        else:
            staged([s for i in range(items) for s in steps(i)], score, top, power, mix)

    block_size = 256
    row_starts = list(range(0, items * SEQ, block_size))
    piece = min(768, ff)
    pieces = list(range(0, ff, piece))

    def first_norm():
        def project(r, _):
            return mm(ctx[pl.ds(r, block_size), :], wo[...])

        def finish(r, attn):
            rows = pl.ds(r, block_size)
            normed, inverse = norm(xp[rows, :].astype(f32) + attn)
            hid[rows, :] = normed * gain_ref[pl.ds(0, 1), :] + bias_ref[pl.ds(0, 1), :]
            if r == 0:
                normed_one[...] = normed
                inverses[0] = jnp.broadcast_to(inverse, inverses.shape[1:])

        staged(row_starts, project, finish)

    def second_norm(total, keep):
        normed, inverse = norm(total)
        if keep:
            normed_two[...] = normed
            inverses[1] = jnp.broadcast_to(inverse, inverses.shape[1:])
        return (normed * gain_ref[pl.ds(1, 1), :] + bias_ref[pl.ds(1, 1), :]).astype(bf16)

    def feed_forward(blocks, size, keep, done):
        def widen(step, _):
            return mm(hid[blocks[step[0]], :].astype(bf16), wup[:, pl.ds(step[1], piece)])

        def activate(step, inner):
            share = 0.5 + 0.5 * lax.erf(inner * ROOT_HALF)
            if keep:
                slope[:, pl.ds(step[1], piece)] = share + inner * (
                    GAUSS * jnp.exp(-0.5 * inner * inner)
                )
            return (inner * share).astype(bf16)

        def narrow(step, active):
            n, s = step
            total = branch.at[n % 2, pl.ds(0, size)]
            start = hid[blocks[n], :] if s == 0 else total[...]
            total[...] = start + mm(active, wdown[pl.ds(s, piece), :])

        def finish(step, _):
            n, s = step
            if s + piece >= ff:
                done(n, second_norm(branch[n % 2, pl.ds(0, size), :], keep))

        steps = [(n, s) for n in range(len(blocks)) for s in pieces]
        staged(steps, widen, activate, narrow, finish)

    def slots_feed_forward():
        def done(_, mixed):
            for i in range(items):
                mixed_p[i, pl.ds(0, slots), :] = mixed[i * slots : (i + 1) * slots]

        feed_forward([pl.ds(0, n_masked)], n_masked, True, done)

    def rest_feed_forward():
        def keep_item(i, mixed):
            mixed_p[i, pl.ds(slots, rest), :] = mixed

        if LOOPS["ffn"]:
            each(
                items,
                lambda i: feed_forward(
                    [rows_at(n_masked, i, rest)], rest, False, lambda _, mixed: keep_item(i, mixed)
                ),
            )
        else:
            feed_forward(
                [rows_at(n_masked, i, rest) for i in range(items)], rest, False, keep_item
            )

    def rows_back():
        upstream = []
        for i in range(items):
            live = lax.broadcasted_iota(jnp.int32, (slots, 1), 0) < count_ref[0:1, i : i + 1]
            picked = t_mm(mt[i, :, pl.ds(0, slots)], cot[pl.ds(i * SEQ, SEQ), :])
            upstream.append(jnp.where(live, picked, 0.0))
        grad_out = jnp.concatenate(upstream, axis=0)
        grad_two = norm_back(
            grad_out * gain_ref[pl.ds(1, 1), :], normed_two[...], inverses[1][:, :1]
        )
        grad_two_low = grad_two.astype(bf16)
        grad_sum = branch.at[0, pl.ds(0, n_masked)]
        grad_sum[...] = grad_two

        def widen(s, _):
            return mm_t(grad_two_low, wdown[pl.ds(s, piece), :])

        def activate(s, grad_active):
            return (slope[:, pl.ds(s, piece)] * grad_active).astype(bf16)

        def narrow(s, grad_inner):
            grad_sum[...] = grad_sum[...] + mm_t(grad_inner, wup[:, pl.ds(s, piece)])

        staged(pieces, widen, activate, narrow)
        grad_one[...] = norm_back(
            grad_sum[...] * gain_ref[pl.ds(0, 1), :], normed_one[...], inverses[0][:, :1]
        )
        grad_context[...] = mm_t(grad_one[...].astype(bf16), wo[...]).astype(bf16)

    def attention_back():
        def where(step):
            i, h, c = step
            return rows_at(0, i, slots), pl.ds((h * pairs_half + c) * PAIR, PAIR)

        def share_of(step):
            i, h, c = step
            return probs[(i * 2 + h) * pairs_half + c]

        def upstream(step, _):
            return mm_t(halves(grad_context[where(step)]), pair_refs(*step)[1][...])

        def scores(step, grad_probs):
            share = share_of(step)
            inner = jnp.sum(share * grad_probs, axis=-1, keepdims=True)
            return (share * (grad_probs - inner)).astype(bf16), share.astype(bf16)

        def products(step, held):
            i, h, c = step
            grad_scores, share_low = held
            keys = pair_refs(*step)[0][...]
            gq[where(step)] = (joined(mm(grad_scores, keys)) * eighth).astype(bf16)
            item_rows = rows_at(0, i, SEQ)
            gkv[h, item_rows, pl.ds(c * PAIR, PAIR)] = (
                mm(halves_across(q8[where(step)]), grad_scores).astype(bf16).T
            )
            gkv[h, item_rows, pl.ds(half + c * PAIR, PAIR)] = (
                mm(halves_across(grad_context[where(step)]), share_low).astype(bf16).T
            )

        def steps(i):
            return [(i, h, c) for h in range(2) for c in range(pairs_half)]

        if LOOPS["aback"]:
            each(items, lambda i: staged(steps(i), upstream, scores, products))
        else:
            staged([s for i in range(items) for s in steps(i)], upstream, scores, products)

    to_sibling = pltpu.make_async_remote_copy(
        src_ref=part_out,
        dst_ref=part_in,
        send_sem=part_sem.at[0],
        recv_sem=part_sem.at[1],
        device_id=sibling,
        device_id_type=MESH,
    )

    def adapter_parts():
        q_part = t_mm(red_q[pl.ds(0, n_masked), :], gq[...])
        part_own[...] = q_part[:, :half] + t_mm(red_v[...], gkv[0, :, pl.ds(half, half)])
        part_out[...] = q_part[:, half:] + t_mm(red_v[...], gkv[1, :, pl.ds(half, half)])

    block_rows = recv_block.shape[1]

    def block_of(j):
        return send_block.at[pl.ds(lax.div(j * RANKS, n_dp), block_rows)]

    def peer_copy(j):
        peer = lax.rem(me + j, n_dp)
        return pltpu.make_async_remote_copy(
            src_ref=block_of(peer),
            dst_ref=recv_block.at[me],
            send_sem=peer_send_sem.at[j],
            recv_sem=peer_recv_sem.at[j],
            device_id={"dp": peer},
            device_id_type=MESH,
        )

    own_copy = pltpu.make_async_copy(block_of(me), recv_block.at[me], part_sem.at[2])

    def send_peers():
        summed = part_own[...] + part_in[...]
        for r in range(RANKS):
            for g in range(pairs_half):
                send_block[r, pl.ds(g, 1), :] = summed[r : r + 1, g * PAIR : (g + 1) * PAIR]

        def start(j, c):
            peer_copy(j).start()
            return c

        lax.fori_loop(1, n_dp, start, 0)
        own_copy.start()

    def wait_peers():
        own_copy.wait()

        def one(j, c):
            peer_copy(j).wait()
            return c

        lax.fori_loop(1, n_dp, one, 0)

    def slots_gradient():
        reduced = high_and_low(2.0 * mm_t(gq[...], adapter_rows(both_b[...], True)))
        compact[...] = (
            grad_one[...] + mm_t(gq[...], wq[...]) + mm(reduced, maps_twice(a_ref[...]))
        ).astype(bf16)

    keep_weights = pltpu.make_async_copy(wkv, wkv_out, part_sem.at[3])

    load_halves()
    greet()
    wait(loads, "pos")
    order(0)
    wait(loads, "x", "a", "b", "k", "v")
    stack_b(0)
    reduced = [reduce_rows(i) for i in range(items)]
    project_kv(0, 0)
    order(1)
    project_kv(0, 1)
    for i in range(items):
        reorder(i, reduced[i])
    wait(loads, "q")
    project_q(0)
    pl.semaphore_wait(barrier, n_dp)
    send_halves()
    attention(0)
    wait(gets, "b", "k", "v")
    keep_weights.start()
    stack_b(1)
    each(items, lambda i: project_kv(1, i), LOOPS["kv"])
    wait(gets, "q")
    project_q(1)
    attention(1)
    wait(loads, "o", "gain", "bias", "count")
    wait(gets, "o")
    first_norm()
    wait(loads, "up", "down", "cot")
    wait(gets, "up", "down")
    slots_feed_forward()
    rows_back()
    attention_back()
    adapter_parts()
    to_sibling.start()
    slots_gradient()
    to_sibling.wait()
    send_peers()
    rest_feed_forward()
    keep_weights.wait()
    wait_peers()


def output_kernel(
    items,
    slots,
    width,
    a_ref,
    mt,
    wkv,
    gkv,
    compact,
    mixed_p,
    both_b,
    recv_block,
    mixed_hbm,
    tg_hbm,
    adapter_hbm,
    mixed,
    tg,
    adapter,
    sem,
):
    half = width // 2

    def adapter_sum():
        total = jnp.sum(recv_block[...], axis=0)
        for r in range(total.shape[0]):
            for g in range(half // PAIR):
                for e in range(2):
                    adapter[pl.ds(2 * g + e, 1), pl.ds(r * HEAD_SIZE, HEAD_SIZE)] = total[
                        r, g : g + 1, e * HEAD_SIZE : (e + 1) * HEAD_SIZE
                    ]

    block_size = 256
    per_item = SEQ // block_size

    def out_copy(n, src, dst, first):
        rows = rows_at(0, n, block_size)
        return pltpu.make_async_copy(src.at[rows], dst.at[rows], sem.at[first + n])

    def token_gradient():
        v_rows = adapter_rows(both_b[...], False)
        maps = maps_twice(a_ref[...])

        def reduce_rows(step, _):
            rows = rows_at(0, step[0] * per_item + step[1], block_size)
            return mm_t(gkv[0, rows, pl.ds(half, half)], v_rows[:, :half]) + mm_t(
                gkv[1, rows, pl.ds(half, half)], v_rows[:, half:]
            )

        def whole(step, reduced):
            i, r = step
            rows = rows_at(0, i * per_item + r, block_size)
            left = jnp.concatenate(
                [
                    mt[i, pl.ds(r * block_size, block_size), pl.ds(0, slots)],
                    high_and_low(2.0 * reduced),
                ],
                axis=1,
            )
            right = jnp.concatenate([compact[rows_at(0, i, slots), :], maps], axis=0)
            tg[rows, :] = (
                mm_t(gkv[0, rows, :], wkv[0]) + mm_t(gkv[1, rows, :], wkv[1]) + mm(left, right)
            )
            out_copy(i * per_item + r, tg, tg_hbm, 1).start()

        def steps(i):
            return [(i, r) for r in range(per_item)]

        if LOOPS["tg"]:
            each(items, lambda i: staged(steps(i), reduce_rows, whole))
        else:
            staged([s for i in range(items) for s in steps(i)], reduce_rows, whole)

    def output_rows():
        def one(i):
            for r in range(per_item):
                n = i * per_item + r
                mixed[rows_at(0, n, block_size), :] = mm(
                    mt[i, pl.ds(r * block_size, block_size), :], mixed_p[i]
                ).astype(bf16)
                out_copy(n, mixed, mixed_hbm, 1 + items * per_item).start()

        each(items, one, LOOPS["out"])

    sums = pltpu.make_async_copy(adapter, adapter_hbm, sem.at[0])
    adapter_sum()
    sums.start()
    token_gradient()
    output_rows()
    sums.wait()
    for n in range(items * per_item):
        out_copy(n, tg, tg_hbm, 1).wait()
        out_copy(n, mixed, mixed_hbm, 1 + items * per_item).wait()


def local(
    tokens,
    query_key_value_weight,
    output_matrix,
    up_matrix,
    down_matrix,
    adapter_down_maps,
    adapter_up_maps,
    layer_norm_gains,
    layer_norm_bias,
    cotangent,
    maskable_positions,
    masked_count_per_item,
    *,
    n_dp,
):
    rows, width = tokens.shape
    items, slots = maskable_positions.shape
    ff = 2 * up_matrix.shape[1]
    half = width // 2
    n_masked = items * slots
    pairs = width // PAIR
    block_rows = max(1, RANKS // n_dp)
    heads = half // HEAD_SIZE
    hbm = pl.BlockSpec(memory_space=pltpu.HBM)
    vmem = pl.BlockSpec(memory_space=pltpu.VMEM)
    a_maps = adapter_down_maps.T
    handed = pl.pallas_call(
        functools.partial(layer_kernel, n_dp, items, slots, width, ff),
        out_shape=(
            pltpu.VMEM((items, SEQ, SEQ), bf16),
            pltpu.VMEM((2, width, width), bf16),
            pltpu.VMEM((2, rows, width), bf16),
            pltpu.VMEM((n_masked, width), bf16),
            pltpu.VMEM((items, SEQ, width), bf16),
            pltpu.VMEM((RANKS, width), bf16),
            pltpu.VMEM((n_dp, block_rows, 8, PAIR), f32),
        ),
        in_specs=[hbm] * 12,
        out_specs=(vmem,) * 7,
        scratch_shapes=[
            pltpu.VMEM((RANKS, width), bf16),
            pltpu.VMEM((2, width), f32),
            pltpu.VMEM((2, width), f32),
            pltpu.VMEM((items, slots), jnp.int32),
            pltpu.VMEM((1, items), jnp.int32),
            pltpu.VMEM((rows, width), bf16),
            pltpu.VMEM((rows, width), bf16),
            pltpu.VMEM((width, width), bf16),
            pltpu.VMEM((2, width, width), bf16),
            pltpu.VMEM((width, width), bf16),
            pltpu.VMEM((width, ff), bf16),
            pltpu.VMEM((ff, width), bf16),
            pltpu.VMEM((2, 2, ADAPTER_RANK, half), bf16),
            pltpu.VMEM((rows, width), bf16),
            pltpu.VMEM((rows, RANKS), bf16),
            pltpu.VMEM((rows, RANKS), bf16),
            pltpu.VMEM((2, rows, width), bf16),
            pltpu.VMEM((rows, width), bf16),
            pltpu.VMEM((rows, width), bf16),
            pltpu.VMEM((items * pairs, 2 * slots, SEQ), f32),
            pltpu.VMEM((rows, width), f32),
            pltpu.VMEM((n_masked, width), f32),
            pltpu.VMEM((n_masked, width), f32),
            pltpu.VMEM((2, n_masked, 128), f32),
            pltpu.VMEM((n_masked, ff), f32),
            pltpu.VMEM((2, max(n_masked, SEQ - slots), width), f32),
            pltpu.VMEM((n_masked, width), bf16),
            pltpu.VMEM((n_masked, width), f32),
            pltpu.VMEM((n_masked, width), bf16),
            pltpu.VMEM((RANKS, half), f32),
            pltpu.VMEM((RANKS, half), f32),
            pltpu.VMEM((RANKS, half), f32),
            pltpu.VMEM((RANKS, 8, PAIR), f32),
            pltpu.SemaphoreType.DMA((14,)),
            pltpu.SemaphoreType.DMA((7,)),
            pltpu.SemaphoreType.DMA((7,)),
            pltpu.SemaphoreType.DMA((4,)),
            pltpu.SemaphoreType.DMA((n_dp,)),
            pltpu.SemaphoreType.DMA((n_dp,)),
        ],
        compiler_params=pltpu.CompilerParams(
            collective_id=0, has_side_effects=True, vmem_limit_bytes=50 * 2**20
        ),
    )(
        tokens,
        query_key_value_weight,
        output_matrix,
        up_matrix,
        down_matrix,
        a_maps,
        adapter_up_maps,
        layer_norm_gains,
        layer_norm_bias,
        cotangent,
        maskable_positions,
        masked_count_per_item.reshape(1, items),
    )
    mixed, token_gradient, by_head = pl.pallas_call(
        functools.partial(output_kernel, items, slots, width),
        out_shape=(
            jax.ShapeDtypeStruct((rows, width), bf16),
            jax.ShapeDtypeStruct((rows, width), f32),
            jax.ShapeDtypeStruct((heads, block_rows * HEAD_SIZE), f32),
        ),
        in_specs=[vmem] * 8,
        out_specs=(hbm,) * 3,
        scratch_shapes=[
            pltpu.VMEM((rows, width), bf16),
            pltpu.VMEM((rows, width), f32),
            pltpu.VMEM((heads, block_rows * HEAD_SIZE), f32),
            pltpu.SemaphoreType.DMA((4 * rows // SEQ + 1,)),
        ],
        compiler_params=pltpu.CompilerParams(vmem_limit_bytes=30 * 2**20),
    )(a_maps, *handed)
    share = RANKS * HEAD_SIZE // n_dp
    if share < HEAD_SIZE:
        at = lax.rem(lax.axis_index("dp"), HEAD_SIZE // share) * share
        by_head = lax.dynamic_slice(by_head, (0, at), (heads, share))
    return mixed, token_gradient, by_head


def solution(mesh):
    return jax.shard_map(
        functools.partial(local, n_dp=mesh.shape["dp"]),
        mesh=mesh,
        in_specs=(
            P(("dp", "tensor"), None),
            P(None, None, "tensor"),
            P("tensor", None),
            P(None, "tensor"),
            P("tensor", None),
            P(),
            P(None, None, "tensor"),
            P(),
            P(),
            P(("dp", "tensor"), None),
            P(("dp", "tensor"), None),
            P(("dp", "tensor")),
        ),
        out_specs=(P(("dp", "tensor"), None), P(("dp", "tensor"), None), P("tensor", "dp")),
        check_vma=False,
    )
```

```python
import functools

import jax
import jax.numpy as jnp
import numpy as np
from jax import lax
from jax.experimental import pallas as pl
from jax.experimental.pallas import tpu as pltpu
from jax.sharding import PartitionSpec as P

HEAD_SIZE = 64
ADAPTER_RANK = 8
RANKS = 2 * ADAPTER_RANK
SEQ = 512
PAIR = 2 * HEAD_SIZE
NORM_EPS = 1e-05
ROOT_HALF = np.float32(0.5**0.5)
GAUSS = np.float32(1.0 / np.sqrt(2.0 * np.pi))
MESH = pl.DeviceIdType.MESH
bf16 = jnp.bfloat16
f32 = jnp.float32


def mm(left, right):
    return jnp.dot(left, right, preferred_element_type=f32)


def mm_t(left, right):
    return lax.dot_general(left, right, (((1,), (1,)), ((), ())), preferred_element_type=f32)


def t_mm(left, right):
    return lax.dot_general(left, right, (((0,), (0,)), ((), ())), preferred_element_type=f32)


def norm(values):
    centre = values - jnp.mean(values, axis=-1, keepdims=True)
    inverse = lax.rsqrt(jnp.mean(centre * centre, axis=-1, keepdims=True) + NORM_EPS)
    return centre * inverse, inverse


def norm_back(scaled, normed, inverse):
    centred = scaled - jnp.mean(scaled, axis=-1, keepdims=True)
    return inverse * (centred - normed * jnp.mean(scaled * normed, axis=-1, keepdims=True))


def staged(steps, *stages):
    held = [None] * len(steps)

    def call(n, stage):
        held[n] = stage(steps[n], held[n])

    return [
        functools.partial(call, t - n, stage)
        for t in range(len(steps) + len(stages) - 1)
        for n, stage in enumerate(stages)
        if 0 <= t - n < len(steps)
    ]


def run(calls):
    for call in calls:
        call()


def between(calls, others):
    merged, done = [], 0
    for n, call in enumerate(calls):
        merged.append(call)
        upto = (n + 1) * len(others) // len(calls)
        merged += others[done:upto]
        done = upto
    return merged


def each(count, body):
    def one(n, c):
        body(n)
        return c

    lax.fori_loop(0, count, one, 0)


def rows_at(first, n, size):
    start = first + n * size
    return pl.ds(start if isinstance(start, int) else pl.multiple_of(start, 128), size)


def halves(block):
    low = lax.broadcasted_iota(jnp.int32, block.shape, 1) < HEAD_SIZE
    zero = jnp.zeros_like(block)
    return jnp.concatenate([jnp.where(low, block, zero), jnp.where(low, zero, block)], axis=0)


def halves_across(block):
    turned = block.T
    low = lax.broadcasted_iota(jnp.int32, turned.shape, 0) < HEAD_SIZE
    zero = jnp.zeros_like(turned)
    return jnp.concatenate([jnp.where(low, turned, zero), jnp.where(low, zero, turned)], axis=1)


def joined(both):
    n = both.shape[0] // 2
    low = lax.broadcasted_iota(jnp.int32, (n, PAIR), 1) < HEAD_SIZE
    return jnp.where(low, both[:n], both[n:])


def adapter_rows(both_b, first):
    is_first = lax.broadcasted_iota(jnp.int32, both_b.shape, 0) < ADAPTER_RANK
    rows = jnp.where(is_first == first, both_b, jnp.zeros_like(both_b))
    blank = jnp.zeros((128 - 2 * RANKS, both_b.shape[1]), bf16)
    return jnp.concatenate([rows, rows, blank], axis=0)


def high_and_low(twice):
    high = twice.astype(bf16)
    low = (twice - high.astype(f32)).astype(bf16)
    column = lax.broadcasted_iota(jnp.int32, twice.shape, 1)
    return jnp.where(column < RANKS, high, low)


def maps_twice(a):
    blank = jnp.zeros((128 - 2 * RANKS, a.shape[1]), bf16)
    return jnp.concatenate([a, a, blank], axis=0)


def token_gradient(blocks, size, a_ref, mt, wkv, gkv, compact, both_b, finish):
    half = wkv.shape[2] // 2
    slots = compact.shape[0] // mt.shape[0]
    v_rows = adapter_rows(both_b[...], False)
    maps = maps_twice(a_ref[...])

    def reduce_rows(n, _):
        rows = rows_at(0, n, size)
        return mm_t(gkv[0, rows, pl.ds(half, half)], v_rows[:, :half]) + mm_t(
            gkv[1, rows, pl.ds(half, half)], v_rows[:, half:]
        )

    def whole(n, reduced):
        i, r = divmod(n * size, SEQ)
        rows = rows_at(0, n, size)
        left = jnp.concatenate(
            [mt[i, pl.ds(r, size), pl.ds(0, slots)], high_and_low(2.0 * reduced)], axis=1
        )
        right = jnp.concatenate([compact[rows_at(0, i, slots), :], maps], axis=0)
        finish(n, mm_t(gkv[0, rows, :], wkv[0]) + mm_t(gkv[1, rows, :], wkv[1]) + mm(left, right))

    return staged(list(blocks), reduce_rows, whole)


def layer_kernel(
    n_dp,
    items,
    slots,
    width,
    ff,
    tokens_hbm,
    qkv_hbm,
    o_hbm,
    up_hbm,
    down_hbm,
    a_hbm,
    b_hbm,
    gain_hbm,
    bias_hbm,
    cot_hbm,
    pos_hbm,
    count_hbm,
    mt,
    wkv,
    gkv,
    compact,
    mixed_p,
    both_b,
    recv_block,
    tg_first,
    a_ref,
    gain_ref,
    bias_ref,
    pos_ref,
    count_ref,
    x,
    xp,
    wq,
    wo,
    wup,
    wdown,
    bmat,
    cot,
    red_q,
    red_v,
    kv,
    q8,
    ctx,
    probs,
    hid,
    normed_one,
    normed_two,
    inverses,
    slope,
    branch,
    grad_sum,
    gq,
    grad_one,
    grad_context,
    part_own,
    part_out,
    part_in,
    send_block,
    load_sem,
    send_sem,
    recv_sem,
    part_sem,
):
    half = width // 2
    half_ff = ff // 2
    pairs_half = half // PAIR
    rest = SEQ - slots
    n_masked = items * slots
    me = lax.axis_index("dp")
    core = lax.axis_index("tensor")
    sibling = {"tensor": 1 - core}
    loads = {}
    gets = {}

    def load(name, src, dst):
        loads[name] = pltpu.make_async_copy(src, dst, load_sem.at[len(loads)])
        loads[name].start()

    def load_rows():
        load("pos", pos_hbm, pos_ref)
        load("a", a_hbm, a_ref)
        load("x", tokens_hbm, x)

    def load_halves():
        load("k", qkv_hbm.at[1], wkv.at[0, :, pl.ds(0, half)])
        load("v", qkv_hbm.at[2], wkv.at[0, :, pl.ds(half, half)])
        load("b", b_hbm, bmat.at[0])
        load("q", qkv_hbm.at[0], wq.at[:, pl.ds(0, half)])
        load("count", count_hbm, count_ref)
        load("cot", cot_hbm, cot)
        load("gain", gain_hbm, gain_ref)
        load("bias", bias_hbm, bias_ref)
        load("o", o_hbm, wo.at[pl.ds(0, half)])
        load("up", up_hbm, wup.at[:, pl.ds(0, half_ff)])
        load("down", down_hbm, wdown.at[pl.ds(0, half_ff)])

    barrier = pltpu.get_barrier_semaphore()

    def greet():
        pl.semaphore_signal(barrier, inc=1, device_id=sibling, device_id_type=MESH)

        def one(j, c):
            peer = lax.rem(me + j, n_dp)
            pl.semaphore_signal(barrier, inc=1, device_id={"dp": peer}, device_id_type=MESH)
            return c

        lax.fori_loop(1, n_dp, one, 0)

    def send(name, src, dst):
        n = len(gets)
        gets[name] = pltpu.make_async_remote_copy(
            src_ref=src,
            dst_ref=dst,
            send_sem=send_sem.at[n],
            recv_sem=recv_sem.at[n],
            device_id=sibling,
            device_id_type=MESH,
        )
        gets[name].start()

    def send_halves():
        send("k", qkv_hbm.at[1], wkv.at[1, :, pl.ds(0, half)])
        send("v", qkv_hbm.at[2], wkv.at[1, :, pl.ds(half, half)])
        send("b", b_hbm, bmat.at[1])
        send("q", qkv_hbm.at[0], wq.at[:, pl.ds(half, half)])
        send("o", o_hbm, wo.at[pl.ds(half, half)])
        send("up", up_hbm, wup.at[:, pl.ds(half_ff, half_ff)])
        send("down", down_hbm, wdown.at[pl.ds(half_ff, half_ff)])

    def wait(*names):
        for name in names:
            loads[name].wait()

    def wait_got(*names):
        for name in names:
            gets[name].wait_recv()

    def order(i):
        place = lax.broadcasted_iota(jnp.int32, (SEQ, slots), 0)
        slot_pos = pos_ref[pl.ds(i, 1), :]
        hit = slot_pos == place
        before = jnp.sum((slot_pos < place).astype(f32), axis=1, keepdims=True)
        taken = jnp.sum(hit.astype(f32), axis=1, keepdims=True)
        own_place = lax.broadcasted_iota(jnp.int32, (SEQ, 1), 0).astype(f32)
        rank = jnp.where(taken > 0.5, -1.0, own_place - before)
        column = lax.broadcasted_iota(jnp.int32, (SEQ, rest), 1).astype(f32)
        mt[i, :, pl.ds(0, slots)] = hit.astype(f32).astype(bf16)
        mt[i, :, pl.ds(slots, rest)] = (rank == column).astype(f32).astype(bf16)

    def rows_of(i):
        return (
            (0, slots, pl.ds(i * slots, slots)),
            (slots, rest, pl.ds(n_masked + i * rest, rest)),
        )

    lane = lax.broadcasted_iota(jnp.int32, (SEQ, RANKS), 1)

    def reduce_rows(i):
        rows = pl.ds(i * SEQ, SEQ)
        doubled = mm_t(x[rows, :], a_ref[...]).astype(bf16) * 2
        zero = jnp.zeros_like(doubled)
        red_v[rows, :] = jnp.where(lane >= ADAPTER_RANK, doubled, zero)
        return jnp.where(lane < ADAPTER_RANK, doubled, zero)

    def reorder(i, reduced):
        ordered = t_mm(mt[i], x[pl.ds(i * SEQ, SEQ), :])
        ordered_red = t_mm(mt[i], reduced)
        for start, size, rows in rows_of(i):
            xp[rows, :] = ordered[start : start + size].astype(bf16)
            red_q[rows, :] = ordered_red[start : start + size].astype(bf16)

    def stack_b(h):
        both_b[:, pl.ds(h * half, half)] = bmat[h].astype(f32).reshape(RANKS, half).astype(bf16)

    def stacked_b(h):
        return both_b[:, pl.ds(h * half, half)]

    def project_kv(h, i):
        rows = rows_at(0, i, SEQ)
        out = mm(x[rows, :], wkv[h])
        kv[h, rows, pl.ds(0, half)] = out[:, :half].astype(bf16)
        kv[h, rows, pl.ds(half, half)] = (
            out[:, half:] + mm(red_v[rows, :], stacked_b(h))
        ).astype(bf16)

    eighth = np.float32(HEAD_SIZE**-0.5)

    def project_q(columns):
        for i in range(items):
            rows = pl.ds(i * SEQ, SEQ)
            out = mm(xp[rows, :], wq[:, columns]) + mm(red_q[rows, :], both_b[:, columns])
            q8[rows, columns] = out.astype(bf16) * eighth.astype(bf16)

    def pair_refs(i, p):
        h, c = divmod(p, pairs_half)
        rows = rows_at(0, i, SEQ)
        return kv.at[h, rows, pl.ds(c * PAIR, PAIR)], kv.at[h, rows, pl.ds(half + c * PAIR, PAIR)]

    def attention(first, last):
        def where(step):
            return step[3], pl.ds(step[1] * PAIR, PAIR)

        def score(step, _):
            return mm_t(halves(q8[where(step)]), pair_refs(step[0], step[1])[0][...])

        def top(step, scores):
            return scores, jnp.max(scores, axis=-1, keepdims=True)

        def power(step, held):
            return jnp.exp(held[0] - held[1])

        def mix(step, expo):
            values = pair_refs(step[0], step[1])[1][...]
            both = mm(expo.astype(bf16), jnp.concatenate([values, jnp.ones_like(values)], axis=1))
            share = 1.0 / both[:, PAIR:]
            ctx[where(step)] = joined(both[:, :PAIR] * share).astype(bf16)
            if step[2] == 0:
                probs[step[0] * 2 * pairs_half + step[1]] = expo * share[:, :1]

        def steps(i):
            starts = [rows_at(0, i, slots)]
            for r in range(0, rest, 128):
                start = n_masked + r + i * rest
                starts.append(pl.ds(start if isinstance(start, int) else pl.multiple_of(start, 128), 128))
            return [(i, p, n, start) for p in range(first, last) for n, start in enumerate(starts)]

        return staged([s for i in range(items) for s in steps(i)], score, top, power, mix)

    block_size = n_masked
    row_starts = list(range(0, items * SEQ, block_size))
    piece = min(768, ff)
    pieces = list(range(0, ff, piece))

    part = block_size // 4
    parts = range(0, block_size, part)

    def project_out(r, _=None):
        return mm(ctx[pl.ds(r, block_size), :], wo[...])

    def first_norm(r, attn):
        def one(p):
            rows = pl.ds(r + p, part)
            normed, inverse = norm(xp[rows, :].astype(f32) + attn[p : p + part])
            hid[rows, :] = normed * gain_ref[pl.ds(0, 1), :] + bias_ref[pl.ds(0, 1), :]
            if r == 0:
                normed_one[rows, :] = normed
                inverses[0, rows, :] = jnp.broadcast_to(inverse, (part, 128))

        return [functools.partial(one, p) for p in parts]

    def second_norm(r):
        def one(p):
            normed, inverse = norm(branch[r // block_size % 2, pl.ds(p, part), :])
            if r == 0:
                normed_two[pl.ds(p, part), :] = normed
                inverses[1, pl.ds(p, part), :] = jnp.broadcast_to(inverse, (part, 128))
            row = r + p
            i, at = divmod(row, slots) if row < n_masked else divmod(row - n_masked, rest)
            if row >= n_masked:
                at += slots
            mixed_p[i, pl.ds(at, part), :] = (
                normed * gain_ref[pl.ds(1, 1), :] + bias_ref[pl.ds(1, 1), :]
            ).astype(bf16)

        return [functools.partial(one, p) for p in parts]

    def feed_forward(starts):
        def widen(step, _):
            r, s = step
            return mm(hid[pl.ds(r, block_size), :].astype(bf16), wup[:, pl.ds(s, piece)])

        def activate(step, inner):
            r, s = step
            share = 0.5 + 0.5 * lax.erf(inner * ROOT_HALF)
            if r == 0:
                slope[:, pl.ds(s, piece)] = share + inner * (GAUSS * jnp.exp(-0.5 * inner * inner))
            return (inner * share).astype(bf16)

        def narrow(step, active):
            r, s = step
            slot = r // block_size % 2
            start = hid[pl.ds(r, block_size), :] if s == 0 else branch[slot]
            branch[slot] = start + mm(active, wdown[pl.ds(s, piece), :])

        return staged([(r, s) for r in starts for s in pieces], widen, activate, narrow)

    def upstream_rows():
        picked = []
        for i in range(items):
            live = lax.broadcasted_iota(jnp.int32, (slots, 1), 0) < count_ref[0:1, i : i + 1]
            rows = t_mm(mt[i, :, pl.ds(0, slots)], cot[pl.ds(i * SEQ, SEQ), :])
            picked.append(jnp.where(live, rows, 0.0))
        grad_one[...] = jnp.concatenate(picked, axis=0)

    def second_norm_back():
        def one(p):
            rows = pl.ds(p, part)
            grad_two = norm_back(
                grad_one[rows, :] * gain_ref[pl.ds(1, 1), :],
                normed_two[rows, :],
                inverses[1, rows, :1],
            )
            grad_context[rows, :] = grad_two.astype(bf16)
            grad_sum[rows, :] = grad_two

        return [functools.partial(one, p) for p in parts]

    def feed_forward_back():
        def widen(s, _):
            return mm_t(grad_context[...], wdown[pl.ds(s, piece), :])

        def activate(s, grad_active):
            return (slope[:, pl.ds(s, piece)] * grad_active).astype(bf16)

        def narrow(s, grad_inner):
            grad_sum[...] = grad_sum[...] + mm_t(grad_inner, wup[:, pl.ds(s, piece)])

        return staged(pieces, widen, activate, narrow)

    def first_norm_back():
        def one(p):
            rows = pl.ds(p, part)
            grad_one[rows, :] = norm_back(
                grad_sum[rows, :] * gain_ref[pl.ds(0, 1), :],
                normed_one[rows, :],
                inverses[0, rows, :1],
            )

        return [functools.partial(one, p) for p in parts]

    def project_back():
        grad_context[...] = mm_t(grad_one[...].astype(bf16), wo[...]).astype(bf16)

    def attention_back():
        def where(step):
            i, p = step
            return rows_at(0, i, slots), pl.ds(p * PAIR, PAIR)

        def share_of(step):
            i, p = step
            return probs[i * 2 * pairs_half + p]

        def upstream(step, _):
            return mm_t(halves(grad_context[where(step)]), pair_refs(*step)[1][...])

        def scores(step, grad_probs):
            share = share_of(step)
            inner = jnp.sum(share * grad_probs, axis=-1, keepdims=True)
            return (share * (grad_probs - inner)).astype(bf16), share.astype(bf16)

        def products(step, held):
            i, p = step
            h, c = divmod(p, pairs_half)
            grad_scores, share_low = held
            keys = pair_refs(*step)[0][...]
            gq[where(step)] = (joined(mm(grad_scores, keys)) * eighth).astype(bf16)
            item_rows = rows_at(0, i, SEQ)
            gkv[h, item_rows, pl.ds(c * PAIR, PAIR)] = (
                mm(halves_across(q8[where(step)]), grad_scores).astype(bf16).T
            )
            gkv[h, item_rows, pl.ds(half + c * PAIR, PAIR)] = (
                mm(halves_across(grad_context[where(step)]), share_low).astype(bf16).T
            )

        def steps(i):
            return [(i, p) for p in range(2 * pairs_half)]

        return staged([s for i in range(items) for s in steps(i)], upstream, scores, products)

    to_sibling = pltpu.make_async_remote_copy(
        src_ref=part_out,
        dst_ref=part_in,
        send_sem=part_sem.at[0],
        recv_sem=part_sem.at[1],
        device_id=sibling,
        device_id_type=MESH,
    )

    def adapter_parts():
        q_part = t_mm(red_q[pl.ds(0, n_masked), :], gq[...])
        part_own[...] = q_part[:, :half] + t_mm(red_v[...], gkv[0, :, pl.ds(half, half)])
        part_out[...] = q_part[:, half:] + t_mm(red_v[...], gkv[1, :, pl.ds(half, half)])

    block_rows = recv_block.shape[1]

    def block_of(j):
        return send_block.at[pl.ds(lax.div(j * RANKS, n_dp), block_rows)]

    def peer_copy(j):
        peer = lax.rem(me + j, n_dp)
        return pltpu.make_async_remote_copy(
            src_ref=block_of(peer),
            dst_ref=recv_block.at[me],
            send_sem=part_sem.at[3],
            recv_sem=part_sem.at[4],
            device_id={"dp": peer},
            device_id_type=MESH,
        )

    own_copy = pltpu.make_async_copy(block_of(me), recv_block.at[me], part_sem.at[2])

    def send_peers():
        summed = part_own[...] + part_in[...]
        for r in range(RANKS):
            for g in range(pairs_half):
                send_block[r, pl.ds(g, 1), :] = summed[r : r + 1, g * PAIR : (g + 1) * PAIR]

        def start(j, c):
            peer_copy(j).start()
            return c

        lax.fori_loop(1, n_dp, start, 0)
        own_copy.start()

    def wait_peers():
        own_copy.wait()

        blocks = recv_block.at[pl.ds(0, n_dp - 1)]
        pltpu.make_async_copy(blocks, blocks, part_sem.at[3]).wait()
        pltpu.make_async_copy(blocks, blocks, part_sem.at[4]).wait()

    def slots_gradient():
        reduced = high_and_low(2.0 * mm_t(gq[...], adapter_rows(both_b[...], True)))
        compact[...] = (
            grad_one[...] + mm_t(gq[...], wq[...]) + mm(reduced, maps_twice(a_ref[...]))
        ).astype(bf16)


    load_rows()
    greet()
    load_halves()
    wait("pos")
    for i in range(items):
        order(i)
    wait("a", "x")
    for i in range(items):
        reorder(i, reduce_rows(i))
    wait("b", "k", "v")
    stack_b(0)
    for i in range(items):
        project_kv(0, i)
    wait("q", "cot", "count")
    project_q(pl.ds(0, half))
    pl.semaphore_wait(barrier, n_dp)
    send_halves()
    run(attention(0, pairs_half))
    upstream_rows()
    wait_got("b", "k", "v", "q")
    stack_b(1)
    for i in range(items):
        project_kv(1, i)
    project_q(pl.ds(half, half))
    run(attention(pairs_half, 2 * pairs_half))
    wait("o", "gain", "bias")
    wait_got("o")

    attn = [project_out(r) for r in row_starts[:2]]
    run(first_norm(0, attn[0]))
    attn += [project_out(r) for r in row_starts[2:]]
    wait("up", "down")
    wait_got("up", "down")
    norms = [call for r, value in zip(row_starts[1:], attn[1:]) for call in first_norm(r, value)]
    run(between(feed_forward(row_starts[:1]), norms))
    wider = feed_forward(row_starts[1:])
    run(between(wider[:4], second_norm(0)))
    run(between(second_norm_back(), wider[4:7]))
    run(feed_forward_back())
    run(between(first_norm_back(), wider[7:11]))
    project_back()
    run(between(attention_back(), wider[11:13]))
    adapter_parts()
    to_sibling.start()
    slots_gradient()
    to_sibling.wait()
    send_peers()

    last = len(pieces) * 3 + 1
    run(wider[13:last])
    run(between(wider[last : 2 * last - 1], second_norm(row_starts[1])))
    run(between(wider[2 * last - 1 :], second_norm(row_starts[2])))
    run(second_norm(row_starts[3]))

    def keep_first(n, value):
        tg_first[rows_at(0, n, 256), :] = value

    first_blocks = range(tg_first.shape[0] // 256)
    run(token_gradient(first_blocks, 256, a_ref, mt, wkv, gkv, compact, both_b, keep_first))
    wait_peers()
    for copy in gets.values():
        copy.wait_send()


def output_kernel(
    items,
    slots,
    width,
    a_ref,
    mt,
    wkv,
    gkv,
    compact,
    mixed_p,
    both_b,
    recv_block,
    tg_first,
    mixed_hbm,
    tg_hbm,
    adapter_hbm,
    mixed,
    tg,
    adapter,
    sem,
):
    half = width // 2

    def adapter_sum():
        total = jnp.sum(recv_block[...], axis=0)
        for r in range(total.shape[0]):
            for g in range(half // PAIR):
                for e in range(2):
                    adapter[pl.ds(2 * g + e, 1), pl.ds(r * HEAD_SIZE, HEAD_SIZE)] = total[
                        r, g : g + 1, e * HEAD_SIZE : (e + 1) * HEAD_SIZE
                    ]

    first_rows = tg_first.shape[0]
    size = 256

    def first_copy():
        return pltpu.make_async_copy(tg_first, tg_hbm.at[pl.ds(0, first_rows)], sem.at[1])

    def tg_copy():
        rows = pl.ds(first_rows, tg.shape[0])
        return pltpu.make_async_copy(tg, tg_hbm.at[rows], sem.at[2])

    def mixed_copy(n):
        rows = pl.ds(n * SEQ, SEQ)
        return pltpu.make_async_copy(mixed.at[rows], mixed_hbm.at[rows], sem.at[3 + n])

    def token_rows():
        def finish(n, value):
            tg[pl.ds(n * size - first_rows, size), :] = value

        blocks = range(first_rows // size, items * SEQ // size)
        run(token_gradient(blocks, size, a_ref, mt, wkv, gkv, compact, both_b, finish))

    def output_rows(i):
        mixed[pl.ds(i * SEQ, SEQ), :] = mm(mt[i], mixed_p[i]).astype(bf16)

    sums = pltpu.make_async_copy(adapter, adapter_hbm, sem.at[0])
    first_copy().start()
    adapter_sum()
    token_rows()
    for i in range(items - 1):
        output_rows(i)
    sums.start()
    tg_copy().start()
    for i in range(items - 1):
        mixed_copy(i).start()
    output_rows(items - 1)
    mixed_copy(items - 1).start()
    sums.wait()
    first_copy().wait()
    tg_copy().wait()
    for i in range(items):
        mixed_copy(i).wait()


def local(
    tokens,
    query_key_value_weight,
    output_matrix,
    up_matrix,
    down_matrix,
    adapter_down_maps,
    adapter_up_maps,
    layer_norm_gains,
    layer_norm_bias,
    cotangent,
    maskable_positions,
    masked_count_per_item,
    *,
    n_dp,
):
    rows, width = tokens.shape
    items, slots = maskable_positions.shape
    ff = 2 * up_matrix.shape[1]
    half = width // 2
    n_masked = items * slots
    pairs = width // PAIR
    block_rows = max(1, RANKS // n_dp)
    heads = half // HEAD_SIZE
    first_rows = items // 2 * SEQ
    hbm = pl.BlockSpec(memory_space=pltpu.HBM)
    vmem = pl.BlockSpec(memory_space=pltpu.VMEM)
    a_maps = adapter_down_maps.T
    handed = pl.pallas_call(
        functools.partial(layer_kernel, n_dp, items, slots, width, ff),
        out_shape=(
            pltpu.VMEM((items, SEQ, SEQ), bf16),
            pltpu.VMEM((2, width, width), bf16),
            pltpu.VMEM((2, rows, width), bf16),
            pltpu.VMEM((n_masked, width), bf16),
            pltpu.VMEM((items, SEQ, width), bf16),
            pltpu.VMEM((RANKS, width), bf16),
            pltpu.VMEM((n_dp, block_rows, 8, PAIR), f32),
            pltpu.VMEM((first_rows, width), f32),
        ),
        in_specs=[hbm] * 12,
        out_specs=(vmem,) * 8,
        scratch_shapes=[
            pltpu.VMEM((RANKS, width), bf16),
            pltpu.VMEM((2, width), f32),
            pltpu.VMEM((2, width), f32),
            pltpu.VMEM((items, slots), jnp.int32),
            pltpu.VMEM((1, items), jnp.int32),
            pltpu.VMEM((rows, width), bf16),
            pltpu.VMEM((rows, width), bf16),
            pltpu.VMEM((width, width), bf16),
            pltpu.VMEM((width, width), bf16),
            pltpu.VMEM((width, ff), bf16),
            pltpu.VMEM((ff, width), bf16),
            pltpu.VMEM((2, 2, ADAPTER_RANK, half), bf16),
            pltpu.VMEM((rows, width), bf16),
            pltpu.VMEM((rows, RANKS), bf16),
            pltpu.VMEM((rows, RANKS), bf16),
            pltpu.VMEM((2, rows, width), bf16),
            pltpu.VMEM((rows, width), bf16),
            pltpu.VMEM((rows, width), bf16),
            pltpu.VMEM((items * pairs, 2 * slots, SEQ), f32),
            pltpu.VMEM((rows, width), f32),
            pltpu.VMEM((n_masked, width), f32),
            pltpu.VMEM((n_masked, width), f32),
            pltpu.VMEM((2, n_masked, 128), f32),
            pltpu.VMEM((n_masked, ff), f32),
            pltpu.VMEM((2, n_masked, width), f32),
            pltpu.VMEM((n_masked, width), f32),
            pltpu.VMEM((n_masked, width), bf16),
            pltpu.VMEM((n_masked, width), f32),
            pltpu.VMEM((n_masked, width), bf16),
            pltpu.VMEM((RANKS, half), f32),
            pltpu.VMEM((RANKS, half), f32),
            pltpu.VMEM((RANKS, half), f32),
            pltpu.VMEM((RANKS, 8, PAIR), f32),
            pltpu.SemaphoreType.DMA((14,)),
            pltpu.SemaphoreType.DMA((7,)),
            pltpu.SemaphoreType.DMA((7,)),
            pltpu.SemaphoreType.DMA((5,)),
        ],
        compiler_params=pltpu.CompilerParams(
            collective_id=0, has_side_effects=True, vmem_limit_bytes=50 * 2**20
        ),
    )(
        tokens,
        query_key_value_weight,
        output_matrix,
        up_matrix,
        down_matrix,
        a_maps,
        adapter_up_maps,
        layer_norm_gains,
        layer_norm_bias,
        cotangent,
        maskable_positions,
        masked_count_per_item.reshape(1, items),
    )
    mixed, token_gradient, by_head = pl.pallas_call(
        functools.partial(output_kernel, items, slots, width),
        out_shape=(
            jax.ShapeDtypeStruct((rows, width), bf16),
            jax.ShapeDtypeStruct((rows, width), f32),
            jax.ShapeDtypeStruct((heads, block_rows * HEAD_SIZE), f32),
        ),
        in_specs=[vmem] * 9,
        out_specs=(hbm,) * 3,
        scratch_shapes=[
            pltpu.VMEM((rows, width), bf16),
            pltpu.VMEM((rows - first_rows, width), f32),
            pltpu.VMEM((heads, block_rows * HEAD_SIZE), f32),
            pltpu.SemaphoreType.DMA((3 + items,)),
        ],
        compiler_params=pltpu.CompilerParams(vmem_limit_bytes=30 * 2**20),
    )(a_maps, *handed)
    share = RANKS * HEAD_SIZE // n_dp
    if share < HEAD_SIZE:
        at = lax.rem(lax.axis_index("dp"), HEAD_SIZE // share) * share
        by_head = lax.dynamic_slice(by_head, (0, at), (heads, share))
    return mixed, token_gradient, by_head


def solution(mesh):
    return jax.shard_map(
        functools.partial(local, n_dp=mesh.shape["dp"]),
        mesh=mesh,
        in_specs=(
            P(("dp", "tensor"), None),
            P(None, None, "tensor"),
            P("tensor", None),
            P(None, "tensor"),
            P("tensor", None),
            P(),
            P(None, None, "tensor"),
            P(),
            P(),
            P(("dp", "tensor"), None),
            P(("dp", "tensor"), None),
            P(("dp", "tensor")),
        ),
        out_specs=(P(("dp", "tensor"), None), P(("dp", "tensor"), None), P("tensor", "dp")),
        check_vma=False,
    )
```

```python
import functools

import jax
import jax.numpy as jnp
import numpy as np
from jax import lax
from jax.experimental import pallas as pl
from jax.experimental.pallas import tpu as pltpu
from jax.sharding import PartitionSpec as P

HEAD_SIZE = 64
ADAPTER_RANK = 8
RANKS = 2 * ADAPTER_RANK
SEQ = 512
PAIR = 2 * HEAD_SIZE
NORM_EPS = 1e-05
ROOT_HALF = np.float32(0.5**0.5)
GAUSS = np.float32(1.0 / np.sqrt(2.0 * np.pi))
MESH = pl.DeviceIdType.MESH
bf16 = jnp.bfloat16
f32 = jnp.float32


def mm(left, right):
    return jnp.dot(left, right, preferred_element_type=f32)


def mm_t(left, right):
    return lax.dot_general(left, right, (((1,), (1,)), ((), ())), preferred_element_type=f32)


def t_mm(left, right):
    return lax.dot_general(left, right, (((0,), (0,)), ((), ())), preferred_element_type=f32)


def norm(values):
    centre = values - jnp.mean(values, axis=-1, keepdims=True)
    inverse = lax.rsqrt(jnp.mean(centre * centre, axis=-1, keepdims=True) + NORM_EPS)
    return centre * inverse, inverse


def norm_back(scaled, normed, inverse):
    centred = scaled - jnp.mean(scaled, axis=-1, keepdims=True)
    return inverse * (centred - normed * jnp.mean(scaled * normed, axis=-1, keepdims=True))


def staged(steps, *stages):
    held = [None] * len(steps)

    def call(n, stage):
        held[n] = stage(steps[n], held[n])

    return [
        functools.partial(call, t - n, stage)
        for t in range(len(steps) + len(stages) - 1)
        for n, stage in enumerate(stages)
        if 0 <= t - n < len(steps)
    ]


def run(calls):
    for call in calls:
        call()


def between(calls, others):
    merged, done = [], 0
    for n, call in enumerate(calls):
        merged.append(call)
        upto = (n + 1) * len(others) // len(calls)
        merged += others[done:upto]
        done = upto
    return merged


def each(count, body):
    def one(n, c):
        body(n)
        return c

    lax.fori_loop(0, count, one, 0)


def rows_at(first, n, size):
    start = first + n * size
    return pl.ds(start if isinstance(start, int) else pl.multiple_of(start, 128), size)


def halves(block):
    low = lax.broadcasted_iota(jnp.int32, block.shape, 1) < HEAD_SIZE
    zero = jnp.zeros_like(block)
    return jnp.concatenate([jnp.where(low, block, zero), jnp.where(low, zero, block)], axis=0)


def halves_across(block):
    turned = block.T
    low = lax.broadcasted_iota(jnp.int32, turned.shape, 0) < HEAD_SIZE
    zero = jnp.zeros_like(turned)
    return jnp.concatenate([jnp.where(low, turned, zero), jnp.where(low, zero, turned)], axis=1)


def joined(both):
    n = both.shape[0] // 2
    low = lax.broadcasted_iota(jnp.int32, (n, PAIR), 1) < HEAD_SIZE
    return jnp.where(low, both[:n], both[n:])


def adapter_rows(both_b, first):
    is_first = lax.broadcasted_iota(jnp.int32, both_b.shape, 0) < ADAPTER_RANK
    rows = jnp.where(is_first == first, both_b, jnp.zeros_like(both_b))
    blank = jnp.zeros((128 - 2 * RANKS, both_b.shape[1]), bf16)
    return jnp.concatenate([rows, rows, blank], axis=0)


def high_and_low(twice):
    high = twice.astype(bf16)
    low = (twice - high.astype(f32)).astype(bf16)
    column = lax.broadcasted_iota(jnp.int32, twice.shape, 1)
    return jnp.where(column < RANKS, high, low)


def maps_twice(a):
    blank = jnp.zeros((128 - 2 * RANKS, a.shape[1]), bf16)
    return jnp.concatenate([a, a, blank], axis=0)


def token_gradient(blocks, size, a_ref, mt, wkv, gkv, compact, both_b, finish):
    half = wkv.shape[2] // 2
    slots = compact.shape[0] // mt.shape[0]
    v_rows = adapter_rows(both_b[...], False)
    maps = maps_twice(a_ref[...])

    def reduce_rows(n, _):
        rows = rows_at(0, n, size)
        return mm_t(gkv[0, rows, pl.ds(half, half)], v_rows[:, :half]) + mm_t(
            gkv[1, rows, pl.ds(half, half)], v_rows[:, half:]
        )

    def whole(n, reduced):
        i, r = divmod(n * size, SEQ)
        rows = rows_at(0, n, size)
        left = jnp.concatenate(
            [mt[i, pl.ds(r, size), pl.ds(0, slots)], high_and_low(2.0 * reduced)], axis=1
        )
        right = jnp.concatenate([compact[rows_at(0, i, slots), :], maps], axis=0)
        finish(n, mm_t(gkv[0, rows, :], wkv[0]) + mm_t(gkv[1, rows, :], wkv[1]) + mm(left, right))

    return staged(list(blocks), reduce_rows, whole)


def layer_kernel(
    n_dp,
    items,
    slots,
    width,
    ff,
    tokens_hbm,
    qkv_hbm,
    o_hbm,
    up_hbm,
    down_hbm,
    a_hbm,
    b_hbm,
    gain_hbm,
    bias_hbm,
    cot_hbm,
    pos_hbm,
    count_hbm,
    mt,
    wkv,
    gkv,
    compact,
    mixed_p,
    both_b,
    recv_block,
    tg_first,
    a_ref,
    gain_ref,
    bias_ref,
    pos_ref,
    count_ref,
    x,
    xp,
    wq,
    wo,
    wup,
    wdown,
    bmat,
    cot,
    red_q,
    red_v,
    kv,
    q8,
    ctx,
    probs,
    hid,
    normed_one,
    normed_two,
    inverses,
    slope,
    branch,
    grad_sum,
    gq,
    grad_one,
    grad_context,
    part_own,
    part_out,
    part_in,
    send_block,
    load_sem,
    send_sem,
    recv_sem,
    part_sem,
):
    half = width // 2
    half_ff = ff // 2
    pairs_half = half // PAIR
    rest = SEQ - slots
    n_masked = items * slots
    me = lax.axis_index("dp")
    core = lax.axis_index("tensor")
    sibling = {"tensor": 1 - core}
    loads = {}
    gets = {}

    def load(name, src, dst):
        loads[name] = pltpu.make_async_copy(src, dst, load_sem.at[len(loads)])
        loads[name].start()

    def load_rows():
        load("pos", pos_hbm, pos_ref)
        load("a", a_hbm, a_ref)
        load("x", tokens_hbm, x)

    def load_halves():
        load("k", qkv_hbm.at[1], wkv.at[0, :, pl.ds(0, half)])
        load("v", qkv_hbm.at[2], wkv.at[0, :, pl.ds(half, half)])
        load("b", b_hbm, bmat.at[0])
        load("q", qkv_hbm.at[0], wq.at[:, pl.ds(0, half)])
        load("count", count_hbm, count_ref)
        load("cot", cot_hbm, cot)
        load("gain", gain_hbm, gain_ref)
        load("bias", bias_hbm, bias_ref)
        load("o", o_hbm, wo.at[pl.ds(0, half)])
        load("up", up_hbm, wup.at[:, pl.ds(0, half_ff)])
        load("down", down_hbm, wdown.at[pl.ds(0, half_ff)])

    barrier = pltpu.get_barrier_semaphore()

    def greet():
        pl.semaphore_signal(barrier, inc=1, device_id=sibling, device_id_type=MESH)

        def one(j, c):
            peer = lax.rem(me + j, n_dp)
            pl.semaphore_signal(barrier, inc=1, device_id={"dp": peer}, device_id_type=MESH)
            return c

        lax.fori_loop(1, n_dp, one, 0)

    def send(name, src, dst):
        n = len(gets)
        gets[name] = pltpu.make_async_remote_copy(
            src_ref=src,
            dst_ref=dst,
            send_sem=send_sem.at[n],
            recv_sem=recv_sem.at[n],
            device_id=sibling,
            device_id_type=MESH,
        )
        gets[name].start()

    def send_halves():
        send("k", qkv_hbm.at[1], wkv.at[1, :, pl.ds(0, half)])
        send("v", qkv_hbm.at[2], wkv.at[1, :, pl.ds(half, half)])
        send("b", b_hbm, bmat.at[1])
        send("q", qkv_hbm.at[0], wq.at[:, pl.ds(half, half)])
        send("o", o_hbm, wo.at[pl.ds(half, half)])
        send("up", up_hbm, wup.at[:, pl.ds(half_ff, half_ff)])
        send("down", down_hbm, wdown.at[pl.ds(half_ff, half_ff)])

    def wait(*names):
        for name in names:
            loads[name].wait()

    def wait_got(*names):
        for name in names:
            gets[name].wait_recv()

    def order(i):
        place = lax.broadcasted_iota(jnp.int32, (SEQ, slots), 0)
        slot_pos = pos_ref[pl.ds(i, 1), :]
        hit = slot_pos == place
        before = jnp.sum((slot_pos < place).astype(f32), axis=1, keepdims=True)
        taken = jnp.sum(hit.astype(f32), axis=1, keepdims=True)
        own_place = lax.broadcasted_iota(jnp.int32, (SEQ, 1), 0).astype(f32)
        rank = jnp.where(taken > 0.5, -1.0, own_place - before)
        column = lax.broadcasted_iota(jnp.int32, (SEQ, rest), 1).astype(f32)
        mt[i, :, pl.ds(0, slots)] = hit.astype(f32).astype(bf16)
        mt[i, :, pl.ds(slots, rest)] = (rank == column).astype(f32).astype(bf16)

    def rows_of(i):
        return (
            (0, slots, pl.ds(i * slots, slots)),
            (slots, rest, pl.ds(n_masked + i * rest, rest)),
        )

    lane = lax.broadcasted_iota(jnp.int32, (SEQ, RANKS), 1)

    def reduce_rows(i):
        rows = pl.ds(i * SEQ, SEQ)
        doubled = mm_t(x[rows, :], a_ref[...]).astype(bf16) * 2
        zero = jnp.zeros_like(doubled)
        red_v[rows, :] = jnp.where(lane >= ADAPTER_RANK, doubled, zero)
        return jnp.where(lane < ADAPTER_RANK, doubled, zero)

    def reorder(i, reduced):
        ordered = t_mm(mt[i], x[pl.ds(i * SEQ, SEQ), :])
        ordered_red = t_mm(mt[i], reduced)
        for start, size, rows in rows_of(i):
            xp[rows, :] = ordered[start : start + size].astype(bf16)
            red_q[rows, :] = ordered_red[start : start + size].astype(bf16)

    def stack_b(h):
        both_b[:, pl.ds(h * half, half)] = bmat[h].astype(f32).reshape(RANKS, half).astype(bf16)

    def stacked_b(h):
        return both_b[:, pl.ds(h * half, half)]

    def project_kv(h, i):
        rows = rows_at(0, i, SEQ)
        out = mm(x[rows, :], wkv[h])
        kv[h, rows, pl.ds(0, half)] = out[:, :half].astype(bf16)
        kv[h, rows, pl.ds(half, half)] = (
            out[:, half:] + mm(red_v[rows, :], stacked_b(h))
        ).astype(bf16)

    eighth = np.float32(HEAD_SIZE**-0.5)

    def project_q(columns):
        def one(i):
            rows = rows_at(0, i, SEQ)
            out = mm(xp[rows, :], wq[:, columns]) + mm(red_q[rows, :], both_b[:, columns])
            q8[rows, columns] = out.astype(bf16) * eighth.astype(bf16)

        each(items, one)

    def pair_refs(i, p):
        h, c = divmod(p, pairs_half)
        rows = rows_at(0, i, SEQ)
        return kv.at[h, rows, pl.ds(c * PAIR, PAIR)], kv.at[h, rows, pl.ds(half + c * PAIR, PAIR)]

    def attention(first, last):
        def where(step):
            return step[3], pl.ds(step[1] * PAIR, PAIR)

        def score(step, _):
            return mm_t(halves(q8[where(step)]), pair_refs(step[0], step[1])[0][...])

        def top(step, scores):
            return scores, jnp.max(scores, axis=-1, keepdims=True)

        def power(step, held):
            return jnp.exp(held[0] - held[1])

        def mix(step, expo):
            values = pair_refs(step[0], step[1])[1][...]
            both = mm(expo.astype(bf16), jnp.concatenate([values, jnp.ones_like(values)], axis=1))
            share = 1.0 / both[:, PAIR:]
            ctx[where(step)] = joined(both[:, :PAIR] * share).astype(bf16)
            if step[2] == 0:
                probs[step[0] * 2 * pairs_half + step[1]] = expo * share[:, :1]

        def steps(i):
            starts = [rows_at(0, i, slots)]
            for r in range(0, rest, 128):
                start = n_masked + r + i * rest
                starts.append(pl.ds(start if isinstance(start, int) else pl.multiple_of(start, 128), 128))
            return [(i, p, n, start) for p in range(first, last) for n, start in enumerate(starts)]

        return staged([s for i in range(items) for s in steps(i)], score, top, power, mix)

    block_size = n_masked
    row_starts = list(range(0, items * SEQ, block_size))
    piece = min(768, ff)
    pieces = list(range(0, ff, piece))

    part = block_size // 4
    parts = range(0, block_size, part)

    def project_out(r, _=None):
        return mm(ctx[pl.ds(r, block_size), :], wo[...])

    def first_norm(r, attn):
        def one(p):
            rows = pl.ds(r + p, part)
            normed, inverse = norm(xp[rows, :].astype(f32) + attn[p : p + part])
            hid[rows, :] = normed * gain_ref[pl.ds(0, 1), :] + bias_ref[pl.ds(0, 1), :]
            if r == 0:
                normed_one[rows, :] = normed
                inverses[0, rows, :] = jnp.broadcast_to(inverse, (part, 128))

        return [functools.partial(one, p) for p in parts]

    def second_norm(r):
        def one(p):
            normed, inverse = norm(branch[r // block_size % 2, pl.ds(p, part), :])
            if r == 0:
                normed_two[pl.ds(p, part), :] = normed
                inverses[1, pl.ds(p, part), :] = jnp.broadcast_to(inverse, (part, 128))
            row = r + p
            i, at = divmod(row, slots) if row < n_masked else divmod(row - n_masked, rest)
            if row >= n_masked:
                at += slots
            mixed_p[i, pl.ds(at, part), :] = (
                normed * gain_ref[pl.ds(1, 1), :] + bias_ref[pl.ds(1, 1), :]
            ).astype(bf16)

        return [functools.partial(one, p) for p in parts]

    def feed_forward(starts):
        def widen(step, _):
            r, s = step
            return mm(hid[pl.ds(r, block_size), :].astype(bf16), wup[:, pl.ds(s, piece)])

        def activate(step, inner):
            r, s = step
            share = 0.5 + 0.5 * lax.erf(inner * ROOT_HALF)
            if r == 0:
                slope[:, pl.ds(s, piece)] = share + inner * (GAUSS * jnp.exp(-0.5 * inner * inner))
            return (inner * share).astype(bf16)

        def narrow(step, active):
            r, s = step
            slot = r // block_size % 2
            start = hid[pl.ds(r, block_size), :] if s == 0 else branch[slot]
            branch[slot] = start + mm(active, wdown[pl.ds(s, piece), :])

        return staged([(r, s) for r in starts for s in pieces], widen, activate, narrow)

    def upstream_rows():
        picked = []
        for i in range(items):
            live = lax.broadcasted_iota(jnp.int32, (slots, 1), 0) < count_ref[0:1, i : i + 1]
            rows = t_mm(mt[i, :, pl.ds(0, slots)], cot[pl.ds(i * SEQ, SEQ), :])
            picked.append(jnp.where(live, rows, 0.0))
        grad_one[...] = jnp.concatenate(picked, axis=0)

    def second_norm_back():
        def one(p):
            rows = pl.ds(p, part)
            grad_two = norm_back(
                grad_one[rows, :] * gain_ref[pl.ds(1, 1), :],
                normed_two[rows, :],
                inverses[1, rows, :1],
            )
            grad_context[rows, :] = grad_two.astype(bf16)
            grad_sum[rows, :] = grad_two

        return [functools.partial(one, p) for p in parts]

    def feed_forward_back():
        def widen(s, _):
            return mm_t(grad_context[...], wdown[pl.ds(s, piece), :])

        def activate(s, grad_active):
            return (slope[:, pl.ds(s, piece)] * grad_active).astype(bf16)

        def narrow(s, grad_inner):
            grad_sum[...] = grad_sum[...] + mm_t(grad_inner, wup[:, pl.ds(s, piece)])

        return staged(pieces, widen, activate, narrow)

    def first_norm_back():
        def one(p):
            rows = pl.ds(p, part)
            grad_one[rows, :] = norm_back(
                grad_sum[rows, :] * gain_ref[pl.ds(0, 1), :],
                normed_one[rows, :],
                inverses[0, rows, :1],
            )

        return [functools.partial(one, p) for p in parts]

    def project_back():
        grad_context[...] = mm_t(grad_one[...].astype(bf16), wo[...]).astype(bf16)

    def attention_back():
        def where(step):
            i, p = step
            return rows_at(0, i, slots), pl.ds(p * PAIR, PAIR)

        def share_of(step):
            i, p = step
            return probs[i * 2 * pairs_half + p]

        def upstream(step, _):
            return mm_t(halves(grad_context[where(step)]), pair_refs(*step)[1][...])

        def scores(step, grad_probs):
            share = share_of(step)
            inner = jnp.sum(share * grad_probs, axis=-1, keepdims=True)
            return (share * (grad_probs - inner)).astype(bf16), share.astype(bf16)

        def products(step, held):
            i, p = step
            h, c = divmod(p, pairs_half)
            grad_scores, share_low = held
            keys = pair_refs(*step)[0][...]
            gq[where(step)] = (joined(mm(grad_scores, keys)) * eighth).astype(bf16)
            item_rows = rows_at(0, i, SEQ)
            gkv[h, item_rows, pl.ds(c * PAIR, PAIR)] = (
                mm(halves_across(q8[where(step)]), grad_scores).astype(bf16).T
            )
            gkv[h, item_rows, pl.ds(half + c * PAIR, PAIR)] = (
                mm(halves_across(grad_context[where(step)]), share_low).astype(bf16).T
            )

        def steps(i):
            return [(i, p) for p in range(2 * pairs_half)]

        return staged([s for i in range(items) for s in steps(i)], upstream, scores, products)

    to_sibling = pltpu.make_async_remote_copy(
        src_ref=part_out,
        dst_ref=part_in,
        send_sem=part_sem.at[0],
        recv_sem=part_sem.at[1],
        device_id=sibling,
        device_id_type=MESH,
    )

    def adapter_parts():
        q_part = t_mm(red_q[pl.ds(0, n_masked), :], gq[...])
        part_own[...] = q_part[:, :half] + t_mm(red_v[...], gkv[0, :, pl.ds(half, half)])
        part_out[...] = q_part[:, half:] + t_mm(red_v[...], gkv[1, :, pl.ds(half, half)])

    block_rows = recv_block.shape[1]

    def block_of(j):
        return send_block.at[pl.ds(lax.div(j * RANKS, n_dp), block_rows)]

    def peer_copy(j):
        peer = lax.rem(me + j, n_dp)
        return pltpu.make_async_remote_copy(
            src_ref=block_of(peer),
            dst_ref=recv_block.at[me],
            send_sem=part_sem.at[3],
            recv_sem=part_sem.at[4],
            device_id={"dp": peer},
            device_id_type=MESH,
        )

    own_copy = pltpu.make_async_copy(block_of(me), recv_block.at[me], part_sem.at[2])

    def send_peers():
        summed = part_own[...] + part_in[...]
        for r in range(RANKS):
            for g in range(pairs_half):
                send_block[r, pl.ds(g, 1), :] = summed[r : r + 1, g * PAIR : (g + 1) * PAIR]

        def start(j, c):
            peer_copy(j).start()
            return c

        lax.fori_loop(1, n_dp, start, 0)
        own_copy.start()

    def wait_peers():
        own_copy.wait()

        blocks = recv_block.at[pl.ds(0, n_dp - 1)]
        pltpu.make_async_copy(blocks, blocks, part_sem.at[3]).wait()
        pltpu.make_async_copy(blocks, blocks, part_sem.at[4]).wait()

    def slots_gradient():
        reduced = high_and_low(2.0 * mm_t(gq[...], adapter_rows(both_b[...], True)))
        compact[...] = (
            grad_one[...] + mm_t(gq[...], wq[...]) + mm(reduced, maps_twice(a_ref[...]))
        ).astype(bf16)


    load_rows()
    greet()
    load_halves()
    wait("pos")
    for i in range(items):
        order(i)
    wait("a", "x")
    for i in range(items):
        reorder(i, reduce_rows(i))
    wait("b", "k", "v")
    stack_b(0)
    each(items, lambda i: project_kv(0, i))
    wait("q", "cot", "count")
    project_q(pl.ds(0, half))
    pl.semaphore_wait(barrier, n_dp)
    send_halves()
    run(attention(0, pairs_half))
    upstream_rows()
    wait_got("b", "k", "v", "q")
    stack_b(1)
    each(items, lambda i: project_kv(1, i))
    project_q(pl.ds(half, half))
    run(attention(pairs_half, 2 * pairs_half))
    wait("o", "gain", "bias")
    wait_got("o")

    attn = [project_out(r) for r in row_starts[:2]]
    run(first_norm(0, attn[0]))
    attn += [project_out(r) for r in row_starts[2:]]
    wait("up", "down")
    wait_got("up", "down")
    norms = [call for r, value in zip(row_starts[1:], attn[1:]) for call in first_norm(r, value)]
    run(between(feed_forward(row_starts[:1]), norms))
    wider = feed_forward(row_starts[1:])
    run(between(wider[:3], second_norm(0)))
    run(between(second_norm_back(), wider[3:4]))
    run(feed_forward_back())
    run(between(first_norm_back(), wider[4:6]))
    project_back()
    run(attention_back())
    adapter_parts()
    to_sibling.start()
    slots_gradient()
    to_sibling.wait()
    send_peers()

    last = len(pieces) * 3 + 1
    run(wider[6:last])
    run(between(wider[last : 2 * last - 1], second_norm(row_starts[1])))
    run(between(wider[2 * last - 1 :], second_norm(row_starts[2])))
    run(second_norm(row_starts[3]))

    def keep_first(n, value):
        tg_first[rows_at(0, n, 256), :] = value

    first_blocks = range(tg_first.shape[0] // 256)
    run(token_gradient(first_blocks, 256, a_ref, mt, wkv, gkv, compact, both_b, keep_first))
    wait_peers()
    for copy in gets.values():
        copy.wait_send()


def output_kernel(
    items,
    slots,
    width,
    a_ref,
    mt,
    wkv,
    gkv,
    compact,
    mixed_p,
    both_b,
    recv_block,
    tg_first,
    mixed_hbm,
    tg_hbm,
    adapter_hbm,
    mixed,
    tg,
    adapter,
    sem,
):
    half = width // 2

    def adapter_sum():
        total = jnp.sum(recv_block[...], axis=0)
        for r in range(total.shape[0]):
            for g in range(half // PAIR):
                for e in range(2):
                    adapter[pl.ds(2 * g + e, 1), pl.ds(r * HEAD_SIZE, HEAD_SIZE)] = total[
                        r, g : g + 1, e * HEAD_SIZE : (e + 1) * HEAD_SIZE
                    ]

    first_rows = tg_first.shape[0]
    size = 256

    def first_copy():
        return pltpu.make_async_copy(tg_first, tg_hbm.at[pl.ds(0, first_rows)], sem.at[1])

    def tg_copy():
        rows = pl.ds(first_rows, tg.shape[0])
        return pltpu.make_async_copy(tg, tg_hbm.at[rows], sem.at[2])

    def mixed_copy(n):
        rows = rows_at(0, n, SEQ)
        return pltpu.make_async_copy(mixed.at[rows], mixed_hbm.at[rows], sem.at[3 + n])

    def token_rows():
        def finish(n, value):
            tg[pl.ds(n * size - first_rows, size), :] = value

        blocks = range(first_rows // size, items * SEQ // size)
        run(token_gradient(blocks, size, a_ref, mt, wkv, gkv, compact, both_b, finish))

    def output_rows(i):
        for r in range(0, SEQ, size):
            rows = pl.ds(pl.multiple_of(i * SEQ + r, size), size)
            mixed[rows, :] = mm(mt[i, pl.ds(r, size), :], mixed_p[i]).astype(bf16)
        mixed_copy(i).start()

    sums = pltpu.make_async_copy(adapter, adapter_hbm, sem.at[0])
    first_copy().start()
    adapter_sum()
    token_rows()
    sums.start()
    tg_copy().start()
    each(items, output_rows)
    sums.wait()
    first_copy().wait()
    tg_copy().wait()
    for i in range(items):
        mixed_copy(i).wait()


def local(
    tokens,
    query_key_value_weight,
    output_matrix,
    up_matrix,
    down_matrix,
    adapter_down_maps,
    adapter_up_maps,
    layer_norm_gains,
    layer_norm_bias,
    cotangent,
    maskable_positions,
    masked_count_per_item,
    *,
    n_dp,
):
    rows, width = tokens.shape
    items, slots = maskable_positions.shape
    ff = 2 * up_matrix.shape[1]
    half = width // 2
    n_masked = items * slots
    pairs = width // PAIR
    block_rows = max(1, RANKS // n_dp)
    heads = half // HEAD_SIZE
    first_rows = items // 2 * SEQ
    hbm = pl.BlockSpec(memory_space=pltpu.HBM)
    vmem = pl.BlockSpec(memory_space=pltpu.VMEM)
    a_maps = adapter_down_maps.T
    handed = pl.pallas_call(
        functools.partial(layer_kernel, n_dp, items, slots, width, ff),
        out_shape=(
            pltpu.VMEM((items, SEQ, SEQ), bf16),
            pltpu.VMEM((2, width, width), bf16),
            pltpu.VMEM((2, rows, width), bf16),
            pltpu.VMEM((n_masked, width), bf16),
            pltpu.VMEM((items, SEQ, width), bf16),
            pltpu.VMEM((RANKS, width), bf16),
            pltpu.VMEM((n_dp, block_rows, 8, PAIR), f32),
            pltpu.VMEM((first_rows, width), f32),
        ),
        in_specs=[hbm] * 12,
        out_specs=(vmem,) * 8,
        scratch_shapes=[
            pltpu.VMEM((RANKS, width), bf16),
            pltpu.VMEM((2, width), f32),
            pltpu.VMEM((2, width), f32),
            pltpu.VMEM((items, slots), jnp.int32),
            pltpu.VMEM((1, items), jnp.int32),
            pltpu.VMEM((rows, width), bf16),
            pltpu.VMEM((rows, width), bf16),
            pltpu.VMEM((width, width), bf16),
            pltpu.VMEM((width, width), bf16),
            pltpu.VMEM((width, ff), bf16),
            pltpu.VMEM((ff, width), bf16),
            pltpu.VMEM((2, 2, ADAPTER_RANK, half), bf16),
            pltpu.VMEM((rows, width), bf16),
            pltpu.VMEM((rows, RANKS), bf16),
            pltpu.VMEM((rows, RANKS), bf16),
            pltpu.VMEM((2, rows, width), bf16),
            pltpu.VMEM((rows, width), bf16),
            pltpu.VMEM((rows, width), bf16),
            pltpu.VMEM((items * pairs, 2 * slots, SEQ), f32),
            pltpu.VMEM((rows, width), f32),
            pltpu.VMEM((n_masked, width), f32),
            pltpu.VMEM((n_masked, width), f32),
            pltpu.VMEM((2, n_masked, 128), f32),
            pltpu.VMEM((n_masked, ff), f32),
            pltpu.VMEM((2, n_masked, width), f32),
            pltpu.VMEM((n_masked, width), f32),
            pltpu.VMEM((n_masked, width), bf16),
            pltpu.VMEM((n_masked, width), f32),
            pltpu.VMEM((n_masked, width), bf16),
            pltpu.VMEM((RANKS, half), f32),
            pltpu.VMEM((RANKS, half), f32),
            pltpu.VMEM((RANKS, half), f32),
            pltpu.VMEM((RANKS, 8, PAIR), f32),
            pltpu.SemaphoreType.DMA((14,)),
            pltpu.SemaphoreType.DMA((7,)),
            pltpu.SemaphoreType.DMA((7,)),
            pltpu.SemaphoreType.DMA((5,)),
        ],
        compiler_params=pltpu.CompilerParams(
            collective_id=0, has_side_effects=True, vmem_limit_bytes=50 * 2**20
        ),
    )(
        tokens,
        query_key_value_weight,
        output_matrix,
        up_matrix,
        down_matrix,
        a_maps,
        adapter_up_maps,
        layer_norm_gains,
        layer_norm_bias,
        cotangent,
        maskable_positions,
        masked_count_per_item.reshape(1, items),
    )
    mixed, token_gradient, by_head = pl.pallas_call(
        functools.partial(output_kernel, items, slots, width),
        out_shape=(
            jax.ShapeDtypeStruct((rows, width), bf16),
            jax.ShapeDtypeStruct((rows, width), f32),
            jax.ShapeDtypeStruct((heads, block_rows * HEAD_SIZE), f32),
        ),
        in_specs=[vmem] * 9,
        out_specs=(hbm,) * 3,
        scratch_shapes=[
            pltpu.VMEM((rows, width), bf16),
            pltpu.VMEM((rows - first_rows, width), f32),
            pltpu.VMEM((heads, block_rows * HEAD_SIZE), f32),
            pltpu.SemaphoreType.DMA((3 + items,)),
        ],
        compiler_params=pltpu.CompilerParams(vmem_limit_bytes=30 * 2**20),
    )(a_maps, *handed)
    share = RANKS * HEAD_SIZE // n_dp
    if share < HEAD_SIZE:
        at = lax.rem(lax.axis_index("dp"), HEAD_SIZE // share) * share
        by_head = lax.dynamic_slice(by_head, (0, at), (heads, share))
    return mixed, token_gradient, by_head


def solution(mesh):
    return jax.shard_map(
        functools.partial(local, n_dp=mesh.shape["dp"]),
        mesh=mesh,
        in_specs=(
            P(("dp", "tensor"), None),
            P(None, None, "tensor"),
            P("tensor", None),
            P(None, "tensor"),
            P("tensor", None),
            P(),
            P(None, None, "tensor"),
            P(),
            P(),
            P(("dp", "tensor"), None),
            P(("dp", "tensor"), None),
            P(("dp", "tensor")),
        ),
        out_specs=(P(("dp", "tensor"), None), P(("dp", "tensor"), None), P("tensor", "dp")),
        check_vma=False,
    )
```

```python
import functools

import jax
import jax.numpy as jnp
import numpy as np
from jax import lax
from jax.experimental import pallas as pl
from jax.experimental.pallas import tpu as pltpu
from jax.sharding import PartitionSpec as P

HEAD_SIZE = 64
ADAPTER_RANK = 8
RANKS = 2 * ADAPTER_RANK
SEQ = 512
PAIR = 2 * HEAD_SIZE
NORM_EPS = 1e-05
ROOT_HALF = np.float32(0.5**0.5)
GAUSS = np.float32(1.0 / np.sqrt(2.0 * np.pi))
MESH = pl.DeviceIdType.MESH
bf16 = jnp.bfloat16
f32 = jnp.float32


def mm(left, right):
    return jnp.dot(left, right, preferred_element_type=f32)


def mm_t(left, right):
    return lax.dot_general(left, right, (((1,), (1,)), ((), ())), preferred_element_type=f32)


def t_mm(left, right):
    return lax.dot_general(left, right, (((0,), (0,)), ((), ())), preferred_element_type=f32)


def norm(values):
    centre = values - jnp.mean(values, axis=-1, keepdims=True)
    inverse = lax.rsqrt(jnp.mean(centre * centre, axis=-1, keepdims=True) + NORM_EPS)
    return centre * inverse, inverse


def norm_back(scaled, normed, inverse):
    centred = scaled - jnp.mean(scaled, axis=-1, keepdims=True)
    return inverse * (centred - normed * jnp.mean(scaled * normed, axis=-1, keepdims=True))


def staged(steps, *stages):
    held = [None] * len(steps)

    def call(n, stage):
        held[n] = stage(steps[n], held[n])

    return [
        functools.partial(call, t - n, stage)
        for t in range(len(steps) + len(stages) - 1)
        for n, stage in enumerate(stages)
        if 0 <= t - n < len(steps)
    ]


def run(calls):
    for call in calls:
        call()


def between(calls, others):
    merged, done = [], 0
    for n, call in enumerate(calls):
        merged.append(call)
        upto = (n + 1) * len(others) // len(calls)
        merged += others[done:upto]
        done = upto
    return merged


def each(count, body):
    def one(n, c):
        body(n)
        return c

    lax.fori_loop(0, count, one, 0)


def rows_at(first, n, size):
    start = first + n * size
    return pl.ds(start if isinstance(start, int) else pl.multiple_of(start, 128), size)


def halves(block):
    low = lax.broadcasted_iota(jnp.int32, block.shape, 1) < HEAD_SIZE
    zero = jnp.zeros_like(block)
    return jnp.concatenate([jnp.where(low, block, zero), jnp.where(low, zero, block)], axis=0)


def halves_across(block):
    turned = block.T
    low = lax.broadcasted_iota(jnp.int32, turned.shape, 0) < HEAD_SIZE
    zero = jnp.zeros_like(turned)
    return jnp.concatenate([jnp.where(low, turned, zero), jnp.where(low, zero, turned)], axis=1)


def joined(both):
    n = both.shape[0] // 2
    low = lax.broadcasted_iota(jnp.int32, (n, PAIR), 1) < HEAD_SIZE
    return jnp.where(low, both[:n], both[n:])


def adapter_rows(both_b, first):
    is_first = lax.broadcasted_iota(jnp.int32, both_b.shape, 0) < ADAPTER_RANK
    rows = jnp.where(is_first == first, both_b, jnp.zeros_like(both_b))
    blank = jnp.zeros((128 - 2 * RANKS, both_b.shape[1]), bf16)
    return jnp.concatenate([rows, rows, blank], axis=0)


def high_and_low(twice):
    high = twice.astype(bf16)
    low = (twice - high.astype(f32)).astype(bf16)
    column = lax.broadcasted_iota(jnp.int32, twice.shape, 1)
    return jnp.where(column < RANKS, high, low)


def maps_twice(a):
    blank = jnp.zeros((128 - 2 * RANKS, a.shape[1]), bf16)
    return jnp.concatenate([a, a, blank], axis=0)


def token_gradient(blocks, size, a_ref, mt, wkv, gkv, compact, both_b, finish):
    half = wkv.shape[2] // 2
    slots = compact.shape[0] // mt.shape[0]
    v_rows = adapter_rows(both_b[...], False)
    maps = maps_twice(a_ref[...])

    def reduce_rows(n, _):
        rows = rows_at(0, n, size)
        return mm_t(gkv[0, rows, pl.ds(half, half)], v_rows[:, :half]) + mm_t(
            gkv[1, rows, pl.ds(half, half)], v_rows[:, half:]
        )

    def whole(n, reduced):
        i, r = divmod(n * size, SEQ)
        rows = rows_at(0, n, size)
        left = jnp.concatenate(
            [mt[i, pl.ds(r, size), pl.ds(0, slots)], high_and_low(2.0 * reduced)], axis=1
        )
        right = jnp.concatenate([compact[rows_at(0, i, slots), :], maps], axis=0)
        finish(n, mm_t(gkv[0, rows, :], wkv[0]) + mm_t(gkv[1, rows, :], wkv[1]) + mm(left, right))

    return staged(list(blocks), reduce_rows, whole)


def layer_kernel(
    n_dp,
    items,
    slots,
    width,
    ff,
    tokens_hbm,
    qkv_hbm,
    o_hbm,
    up_hbm,
    down_hbm,
    a_hbm,
    b_hbm,
    gain_hbm,
    bias_hbm,
    cot_hbm,
    pos_hbm,
    count_hbm,
    mt,
    wkv,
    gkv,
    compact,
    mixed_p,
    both_b,
    recv_block,
    tg_first,
    a_ref,
    gain_ref,
    bias_ref,
    pos_ref,
    count_ref,
    x,
    xp,
    wq,
    wo,
    wup,
    wdown,
    bmat,
    cot,
    red_q,
    red_v,
    kv,
    q8,
    ctx,
    probs,
    hid,
    normed_one,
    normed_two,
    inverses,
    slope,
    branch,
    grad_sum,
    gq,
    grad_one,
    grad_context,
    part_own,
    part_out,
    part_in,
    send_block,
    load_sem,
    send_sem,
    recv_sem,
    part_sem,
):
    half = width // 2
    half_ff = ff // 2
    pairs_half = half // PAIR
    rest = SEQ - slots
    n_masked = items * slots
    me = lax.axis_index("dp")
    core = lax.axis_index("tensor")
    sibling = {"tensor": 1 - core}
    loads = {}
    gets = {}

    def load(name, src, dst):
        loads[name] = pltpu.make_async_copy(src, dst, load_sem.at[len(loads)])
        loads[name].start()

    def load_rows():
        load("pos", pos_hbm, pos_ref)
        load("a", a_hbm, a_ref)
        load("x", tokens_hbm, x)

    def load_halves():
        load("k", qkv_hbm.at[1], wkv.at[0, :, pl.ds(0, half)])
        load("v", qkv_hbm.at[2], wkv.at[0, :, pl.ds(half, half)])
        load("b", b_hbm, bmat.at[0])
        load("q", qkv_hbm.at[0], wq.at[:, pl.ds(0, half)])
        load("count", count_hbm, count_ref)
        load("cot", cot_hbm, cot)
        load("gain", gain_hbm, gain_ref)
        load("bias", bias_hbm, bias_ref)
        load("o", o_hbm, wo.at[pl.ds(0, half)])
        load("up", up_hbm, wup.at[:, pl.ds(0, half_ff)])
        load("down", down_hbm, wdown.at[pl.ds(0, half_ff)])

    barrier = pltpu.get_barrier_semaphore()

    def greet():
        pl.semaphore_signal(barrier, inc=1, device_id=sibling, device_id_type=MESH)

        def one(j, c):
            peer = lax.rem(me + j, n_dp)
            pl.semaphore_signal(barrier, inc=1, device_id={"dp": peer}, device_id_type=MESH)
            return c

        lax.fori_loop(1, n_dp, one, 0)

    def send(name, src, dst):
        n = len(gets)
        gets[name] = pltpu.make_async_remote_copy(
            src_ref=src,
            dst_ref=dst,
            send_sem=send_sem.at[n],
            recv_sem=recv_sem.at[n],
            device_id=sibling,
            device_id_type=MESH,
        )
        gets[name].start()

    def send_halves():
        send("k", qkv_hbm.at[1], wkv.at[1, :, pl.ds(0, half)])
        send("v", qkv_hbm.at[2], wkv.at[1, :, pl.ds(half, half)])
        send("b", b_hbm, bmat.at[1])
        send("q", qkv_hbm.at[0], wq.at[:, pl.ds(half, half)])
        send("o", o_hbm, wo.at[pl.ds(half, half)])
        send("up", up_hbm, wup.at[:, pl.ds(half_ff, half_ff)])
        send("down", down_hbm, wdown.at[pl.ds(half_ff, half_ff)])

    def wait(*names):
        for name in names:
            loads[name].wait()

    def wait_got(*names):
        for name in names:
            gets[name].wait_recv()

    def order(i):
        place = lax.broadcasted_iota(jnp.int32, (SEQ, slots), 0)
        slot_pos = pos_ref[pl.ds(i, 1), :]
        hit = slot_pos == place
        before = jnp.sum((slot_pos < place).astype(f32), axis=1, keepdims=True)
        taken = jnp.sum(hit.astype(f32), axis=1, keepdims=True)
        own_place = lax.broadcasted_iota(jnp.int32, (SEQ, 1), 0).astype(f32)
        rank = jnp.where(taken > 0.5, -1.0, own_place - before)
        column = lax.broadcasted_iota(jnp.int32, (SEQ, rest), 1).astype(f32)
        mt[i, :, pl.ds(0, slots)] = hit.astype(f32).astype(bf16)
        mt[i, :, pl.ds(slots, rest)] = (rank == column).astype(f32).astype(bf16)

    def rows_of(i):
        return (
            (0, slots, pl.ds(i * slots, slots)),
            (slots, rest, pl.ds(n_masked + i * rest, rest)),
        )

    lane = lax.broadcasted_iota(jnp.int32, (SEQ, RANKS), 1)

    def reduce_rows(i):
        rows = pl.ds(i * SEQ, SEQ)
        doubled = mm_t(x[rows, :], a_ref[...]).astype(bf16) * 2
        zero = jnp.zeros_like(doubled)
        red_v[rows, :] = jnp.where(lane >= ADAPTER_RANK, doubled, zero)
        return jnp.where(lane < ADAPTER_RANK, doubled, zero)

    def reorder(i, reduced):
        ordered = t_mm(mt[i], x[pl.ds(i * SEQ, SEQ), :])
        ordered_red = t_mm(mt[i], reduced)
        for start, size, rows in rows_of(i):
            xp[rows, :] = ordered[start : start + size].astype(bf16)
            red_q[rows, :] = ordered_red[start : start + size].astype(bf16)

    def stack_b(h):
        both_b[:, pl.ds(h * half, half)] = bmat[h].astype(f32).reshape(RANKS, half).astype(bf16)

    def stacked_b(h):
        return both_b[:, pl.ds(h * half, half)]

    def project_kv(h, i):
        rows = rows_at(0, i, SEQ)
        out = mm(x[rows, :], wkv[h])
        kv[h, rows, pl.ds(0, half)] = out[:, :half].astype(bf16)
        kv[h, rows, pl.ds(half, half)] = (
            out[:, half:] + mm(red_v[rows, :], stacked_b(h))
        ).astype(bf16)

    eighth = np.float32(HEAD_SIZE**-0.5)

    def project_q(columns, loop):
        def one(i):
            rows = rows_at(0, i, SEQ)
            out = mm(xp[rows, :], wq[:, columns]) + mm(red_q[rows, :], both_b[:, columns])
            q8[rows, columns] = out.astype(bf16) * eighth.astype(bf16)

        if loop:
            each(items, one)
        else:
            for i in range(items):
                one(i)

    def pair_refs(i, p):
        h, c = divmod(p, pairs_half)
        rows = rows_at(0, i, SEQ)
        return kv.at[h, rows, pl.ds(c * PAIR, PAIR)], kv.at[h, rows, pl.ds(half + c * PAIR, PAIR)]

    def attention(first, last):
        def where(step):
            return step[3], pl.ds(step[1] * PAIR, PAIR)

        def score(step, _):
            return mm_t(halves(q8[where(step)]), pair_refs(step[0], step[1])[0][...])

        def top(step, scores):
            return scores, jnp.max(scores, axis=-1, keepdims=True)

        def power(step, held):
            return jnp.exp(held[0] - held[1])

        def mix(step, expo):
            values = pair_refs(step[0], step[1])[1][...]
            both = mm(expo.astype(bf16), jnp.concatenate([values, jnp.ones_like(values)], axis=1))
            share = 1.0 / both[:, PAIR:]
            ctx[where(step)] = joined(both[:, :PAIR] * share).astype(bf16)
            if step[2] == 0:
                probs[step[0] * 2 * pairs_half + step[1]] = expo * share[:, :1]

        def steps(i):
            starts = [rows_at(0, i, slots)]
            for r in range(0, rest, 128):
                start = n_masked + r + i * rest
                starts.append(pl.ds(start if isinstance(start, int) else pl.multiple_of(start, 128), 128))
            return [(i, p, n, start) for p in range(first, last) for n, start in enumerate(starts)]

        return staged([s for i in range(items) for s in steps(i)], score, top, power, mix)

    block_size = n_masked
    row_starts = list(range(0, items * SEQ, block_size))
    piece = min(768, ff)
    pieces = list(range(0, ff, piece))

    part = block_size // 4
    parts = range(0, block_size, part)

    def project_out(r, _=None):
        return mm(ctx[pl.ds(r, block_size), :], wo[...])

    def first_norm(r, attn):
        def one(p):
            rows = pl.ds(r + p, part)
            normed, inverse = norm(xp[rows, :].astype(f32) + attn[p : p + part])
            hid[rows, :] = normed * gain_ref[pl.ds(0, 1), :] + bias_ref[pl.ds(0, 1), :]
            if r == 0:
                normed_one[rows, :] = normed
                inverses[0, rows, :] = jnp.broadcast_to(inverse, (part, 128))

        return [functools.partial(one, p) for p in parts]

    def second_norm(r):
        def one(p):
            normed, inverse = norm(branch[r // block_size % 2, pl.ds(p, part), :])
            if r == 0:
                normed_two[pl.ds(p, part), :] = normed
                inverses[1, pl.ds(p, part), :] = jnp.broadcast_to(inverse, (part, 128))
            row = r + p
            i, at = divmod(row, slots) if row < n_masked else divmod(row - n_masked, rest)
            if row >= n_masked:
                at += slots
            mixed_p[i, pl.ds(at, part), :] = (
                normed * gain_ref[pl.ds(1, 1), :] + bias_ref[pl.ds(1, 1), :]
            ).astype(bf16)

        return [functools.partial(one, p) for p in parts]

    def feed_forward(starts):
        def widen(step, _):
            r, s = step
            return mm(hid[pl.ds(r, block_size), :].astype(bf16), wup[:, pl.ds(s, piece)])

        def activate(step, inner):
            r, s = step
            share = 0.5 + 0.5 * lax.erf(inner * ROOT_HALF)
            if r == 0:
                slope[:, pl.ds(s, piece)] = share + inner * (GAUSS * jnp.exp(-0.5 * inner * inner))
            return (inner * share).astype(bf16)

        def narrow(step, active):
            r, s = step
            slot = r // block_size % 2
            start = hid[pl.ds(r, block_size), :] if s == 0 else branch[slot]
            branch[slot] = start + mm(active, wdown[pl.ds(s, piece), :])

        return staged([(r, s) for r in starts for s in pieces], widen, activate, narrow)

    def upstream_rows():
        picked = []
        for i in range(items):
            live = lax.broadcasted_iota(jnp.int32, (slots, 1), 0) < count_ref[0:1, i : i + 1]
            rows = t_mm(mt[i, :, pl.ds(0, slots)], cot[pl.ds(i * SEQ, SEQ), :])
            picked.append(jnp.where(live, rows, 0.0))
        grad_one[...] = jnp.concatenate(picked, axis=0)

    def second_norm_back():
        def one(p):
            rows = pl.ds(p, part)
            grad_two = norm_back(
                grad_one[rows, :] * gain_ref[pl.ds(1, 1), :],
                normed_two[rows, :],
                inverses[1, rows, :1],
            )
            grad_context[rows, :] = grad_two.astype(bf16)
            grad_sum[rows, :] = grad_two

        return [functools.partial(one, p) for p in parts]

    def feed_forward_back():
        def widen(s, _):
            return mm_t(grad_context[...], wdown[pl.ds(s, piece), :])

        def activate(s, grad_active):
            return (slope[:, pl.ds(s, piece)] * grad_active).astype(bf16)

        def narrow(s, grad_inner):
            grad_sum[...] = grad_sum[...] + mm_t(grad_inner, wup[:, pl.ds(s, piece)])

        return staged(pieces, widen, activate, narrow)

    def first_norm_back():
        def one(p):
            rows = pl.ds(p, part)
            grad_one[rows, :] = norm_back(
                grad_sum[rows, :] * gain_ref[pl.ds(0, 1), :],
                normed_one[rows, :],
                inverses[0, rows, :1],
            )

        return [functools.partial(one, p) for p in parts]

    def project_back():
        grad_context[...] = mm_t(grad_one[...].astype(bf16), wo[...]).astype(bf16)

    def attention_back():
        def where(step):
            i, p = step
            return rows_at(0, i, slots), pl.ds(p * PAIR, PAIR)

        def share_of(step):
            i, p = step
            return probs[i * 2 * pairs_half + p]

        def upstream(step, _):
            return mm_t(halves(grad_context[where(step)]), pair_refs(*step)[1][...])

        def scores(step, grad_probs):
            share = share_of(step)
            inner = jnp.sum(share * grad_probs, axis=-1, keepdims=True)
            return (share * (grad_probs - inner)).astype(bf16), share.astype(bf16)

        def products(step, held):
            i, p = step
            h, c = divmod(p, pairs_half)
            grad_scores, share_low = held
            keys = pair_refs(*step)[0][...]
            gq[where(step)] = (joined(mm(grad_scores, keys)) * eighth).astype(bf16)
            item_rows = rows_at(0, i, SEQ)
            gkv[h, item_rows, pl.ds(c * PAIR, PAIR)] = (
                mm(halves_across(q8[where(step)]), grad_scores).astype(bf16).T
            )
            gkv[h, item_rows, pl.ds(half + c * PAIR, PAIR)] = (
                mm(halves_across(grad_context[where(step)]), share_low).astype(bf16).T
            )

        def steps(i):
            return [(i, p) for p in range(2 * pairs_half)]

        return staged([s for i in range(items) for s in steps(i)], upstream, scores, products)

    to_sibling = pltpu.make_async_remote_copy(
        src_ref=part_out,
        dst_ref=part_in,
        send_sem=part_sem.at[0],
        recv_sem=part_sem.at[1],
        device_id=sibling,
        device_id_type=MESH,
    )

    def adapter_parts():
        q_part = t_mm(red_q[pl.ds(0, n_masked), :], gq[...])
        part_own[...] = q_part[:, :half] + t_mm(red_v[...], gkv[0, :, pl.ds(half, half)])
        part_out[...] = q_part[:, half:] + t_mm(red_v[...], gkv[1, :, pl.ds(half, half)])

    block_rows = recv_block.shape[1]

    def block_of(j):
        return send_block.at[pl.ds(lax.div(j * RANKS, n_dp), block_rows)]

    def peer_copy(j):
        peer = lax.rem(me + j, n_dp)
        return pltpu.make_async_remote_copy(
            src_ref=block_of(peer),
            dst_ref=recv_block.at[me],
            send_sem=part_sem.at[3],
            recv_sem=part_sem.at[4],
            device_id={"dp": peer},
            device_id_type=MESH,
        )

    own_copy = pltpu.make_async_copy(block_of(me), recv_block.at[me], part_sem.at[2])

    def send_peers():
        summed = part_own[...] + part_in[...]
        for r in range(RANKS):
            for g in range(pairs_half):
                send_block[r, pl.ds(g, 1), :] = summed[r : r + 1, g * PAIR : (g + 1) * PAIR]

        def start(j, c):
            peer_copy(j).start()
            return c

        lax.fori_loop(1, n_dp, start, 0)
        own_copy.start()

    def wait_peers():
        own_copy.wait()

        blocks = recv_block.at[pl.ds(0, n_dp - 1)]
        pltpu.make_async_copy(blocks, blocks, part_sem.at[3]).wait()
        pltpu.make_async_copy(blocks, blocks, part_sem.at[4]).wait()

    def slots_gradient():
        reduced = high_and_low(2.0 * mm_t(gq[...], adapter_rows(both_b[...], True)))
        compact[...] = (
            grad_one[...] + mm_t(gq[...], wq[...]) + mm(reduced, maps_twice(a_ref[...]))
        ).astype(bf16)


    load_rows()
    greet()
    load_halves()
    wait("pos")
    for i in range(items):
        order(i)
    wait("a", "x")
    for i in range(items):
        reorder(i, reduce_rows(i))
    wait("b", "k", "v", "q", "cot", "count")
    stack_b(0)
    each(items, lambda i: project_kv(0, i))
    project_q(pl.ds(0, half), True)
    pl.semaphore_wait(barrier, n_dp)
    send_halves()
    run(attention(0, pairs_half))
    upstream_rows()
    wait_got("b", "k", "v", "q")
    stack_b(1)
    for i in range(items):
        project_kv(1, i)
    project_q(pl.ds(half, half), False)
    run(attention(pairs_half, 2 * pairs_half))
    wait("o", "gain", "bias")
    wait_got("o")

    attn = [project_out(r) for r in row_starts[:2]]
    run(first_norm(0, attn[0]))
    attn += [project_out(r) for r in row_starts[2:]]
    wait("up", "down")
    wait_got("up", "down")
    norms = [call for r, value in zip(row_starts[1:], attn[1:]) for call in first_norm(r, value)]
    run(between(feed_forward(row_starts[:1]), norms[: len(parts)]))
    wider = feed_forward(row_starts[1:])
    run(between(wider[:3], second_norm(0)))
    run(between(second_norm_back(), wider[3:4]))
    run(between(feed_forward_back(), norms[len(parts) :]))
    run(between(first_norm_back(), wider[4:6]))
    project_back()
    run(attention_back())
    adapter_parts()
    to_sibling.start()
    slots_gradient()
    run(wider[6:7])
    to_sibling.wait()
    send_peers()

    last = len(pieces) * 3 + 1
    run(wider[7:last])
    run(between(wider[last : 2 * last - 1], second_norm(row_starts[1])))
    run(between(wider[2 * last - 1 :], second_norm(row_starts[2])))
    run(second_norm(row_starts[3]))

    def keep_first(n, value):
        tg_first[rows_at(0, n, 256), :] = value

    first_blocks = range(tg_first.shape[0] // 256)
    run(token_gradient(first_blocks, 256, a_ref, mt, wkv, gkv, compact, both_b, keep_first))
    wait_peers()
    for copy in gets.values():
        copy.wait_send()


def output_kernel(
    items,
    slots,
    width,
    a_ref,
    mt,
    wkv,
    gkv,
    compact,
    mixed_p,
    both_b,
    recv_block,
    tg_first,
    mixed_hbm,
    tg_hbm,
    adapter_hbm,
    mixed,
    tg,
    adapter,
    sem,
):
    half = width // 2

    def adapter_sum():
        total = jnp.sum(recv_block[...], axis=0)
        for r in range(total.shape[0]):
            for g in range(half // PAIR):
                for e in range(2):
                    adapter[pl.ds(2 * g + e, 1), pl.ds(r * HEAD_SIZE, HEAD_SIZE)] = total[
                        r, g : g + 1, e * HEAD_SIZE : (e + 1) * HEAD_SIZE
                    ]

    first_rows = tg_first.shape[0]
    size = 256

    def first_copy():
        return pltpu.make_async_copy(tg_first, tg_hbm.at[pl.ds(0, first_rows)], sem.at[1])

    def tg_copy():
        rows = pl.ds(first_rows, tg.shape[0])
        return pltpu.make_async_copy(tg, tg_hbm.at[rows], sem.at[2])

    def mixed_copy(n):
        rows = rows_at(0, n, SEQ)
        return pltpu.make_async_copy(mixed.at[rows], mixed_hbm.at[rows], sem.at[3 + n])

    def token_rows():
        def finish(n, value):
            tg[pl.ds(n * size - first_rows, size), :] = value

        blocks = range(first_rows // size, items * SEQ // size)
        run(token_gradient(blocks, size, a_ref, mt, wkv, gkv, compact, both_b, finish))

    def output_rows(i):
        for r in range(0, SEQ, size):
            rows = pl.ds(pl.multiple_of(i * SEQ + r, size), size)
            mixed[rows, :] = mm(mt[i, pl.ds(r, size), :], mixed_p[i]).astype(bf16)
        mixed_copy(i).start()

    sums = pltpu.make_async_copy(adapter, adapter_hbm, sem.at[0])
    first_copy().start()
    adapter_sum()
    token_rows()
    sums.start()
    tg_copy().start()
    each(items, output_rows)
    sums.wait()
    first_copy().wait()
    tg_copy().wait()
    for i in range(items):
        mixed_copy(i).wait()


def local(
    tokens,
    query_key_value_weight,
    output_matrix,
    up_matrix,
    down_matrix,
    adapter_down_maps,
    adapter_up_maps,
    layer_norm_gains,
    layer_norm_bias,
    cotangent,
    maskable_positions,
    masked_count_per_item,
    *,
    n_dp,
):
    rows, width = tokens.shape
    items, slots = maskable_positions.shape
    ff = 2 * up_matrix.shape[1]
    half = width // 2
    n_masked = items * slots
    pairs = width // PAIR
    block_rows = max(1, RANKS // n_dp)
    heads = half // HEAD_SIZE
    first_rows = items // 2 * SEQ
    hbm = pl.BlockSpec(memory_space=pltpu.HBM)
    vmem = pl.BlockSpec(memory_space=pltpu.VMEM)
    a_maps = adapter_down_maps.T
    handed = pl.pallas_call(
        functools.partial(layer_kernel, n_dp, items, slots, width, ff),
        out_shape=(
            pltpu.VMEM((items, SEQ, SEQ), bf16),
            pltpu.VMEM((2, width, width), bf16),
            pltpu.VMEM((2, rows, width), bf16),
            pltpu.VMEM((n_masked, width), bf16),
            pltpu.VMEM((items, SEQ, width), bf16),
            pltpu.VMEM((RANKS, width), bf16),
            pltpu.VMEM((n_dp, block_rows, 8, PAIR), f32),
            pltpu.VMEM((first_rows, width), f32),
        ),
        in_specs=[hbm] * 12,
        out_specs=(vmem,) * 8,
        scratch_shapes=[
            pltpu.VMEM((RANKS, width), bf16),
            pltpu.VMEM((2, width), f32),
            pltpu.VMEM((2, width), f32),
            pltpu.VMEM((items, slots), jnp.int32),
            pltpu.VMEM((1, items), jnp.int32),
            pltpu.VMEM((rows, width), bf16),
            pltpu.VMEM((rows, width), bf16),
            pltpu.VMEM((width, width), bf16),
            pltpu.VMEM((width, width), bf16),
            pltpu.VMEM((width, ff), bf16),
            pltpu.VMEM((ff, width), bf16),
            pltpu.VMEM((2, 2, ADAPTER_RANK, half), bf16),
            pltpu.VMEM((rows, width), bf16),
            pltpu.VMEM((rows, RANKS), bf16),
            pltpu.VMEM((rows, RANKS), bf16),
            pltpu.VMEM((2, rows, width), bf16),
            pltpu.VMEM((rows, width), bf16),
            pltpu.VMEM((rows, width), bf16),
            pltpu.VMEM((items * pairs, 2 * slots, SEQ), f32),
            pltpu.VMEM((rows, width), f32),
            pltpu.VMEM((n_masked, width), f32),
            pltpu.VMEM((n_masked, width), f32),
            pltpu.VMEM((2, n_masked, 128), f32),
            pltpu.VMEM((n_masked, ff), f32),
            pltpu.VMEM((2, n_masked, width), f32),
            pltpu.VMEM((n_masked, width), f32),
            pltpu.VMEM((n_masked, width), bf16),
            pltpu.VMEM((n_masked, width), f32),
            pltpu.VMEM((n_masked, width), bf16),
            pltpu.VMEM((RANKS, half), f32),
            pltpu.VMEM((RANKS, half), f32),
            pltpu.VMEM((RANKS, half), f32),
            pltpu.VMEM((RANKS, 8, PAIR), f32),
            pltpu.SemaphoreType.DMA((14,)),
            pltpu.SemaphoreType.DMA((7,)),
            pltpu.SemaphoreType.DMA((7,)),
            pltpu.SemaphoreType.DMA((5,)),
        ],
        compiler_params=pltpu.CompilerParams(
            collective_id=0, has_side_effects=True, vmem_limit_bytes=50 * 2**20
        ),
    )(
        tokens,
        query_key_value_weight,
        output_matrix,
        up_matrix,
        down_matrix,
        a_maps,
        adapter_up_maps,
        layer_norm_gains,
        layer_norm_bias,
        cotangent,
        maskable_positions,
        masked_count_per_item.reshape(1, items),
    )
    mixed, token_gradient, by_head = pl.pallas_call(
        functools.partial(output_kernel, items, slots, width),
        out_shape=(
            jax.ShapeDtypeStruct((rows, width), bf16),
            jax.ShapeDtypeStruct((rows, width), f32),
            jax.ShapeDtypeStruct((heads, block_rows * HEAD_SIZE), f32),
        ),
        in_specs=[vmem] * 9,
        out_specs=(hbm,) * 3,
        scratch_shapes=[
            pltpu.VMEM((rows, width), bf16),
            pltpu.VMEM((rows - first_rows, width), f32),
            pltpu.VMEM((heads, block_rows * HEAD_SIZE), f32),
            pltpu.SemaphoreType.DMA((3 + items,)),
        ],
        compiler_params=pltpu.CompilerParams(vmem_limit_bytes=30 * 2**20),
    )(a_maps, *handed)
    share = RANKS * HEAD_SIZE // n_dp
    if share < HEAD_SIZE:
        at = lax.rem(lax.axis_index("dp"), HEAD_SIZE // share) * share
        by_head = lax.dynamic_slice(by_head, (0, at), (heads, share))
    return mixed, token_gradient, by_head


def solution(mesh):
    return jax.shard_map(
        functools.partial(local, n_dp=mesh.shape["dp"]),
        mesh=mesh,
        in_specs=(
            P(("dp", "tensor"), None),
            P(None, None, "tensor"),
            P("tensor", None),
            P(None, "tensor"),
            P("tensor", None),
            P(),
            P(None, None, "tensor"),
            P(),
            P(),
            P(("dp", "tensor"), None),
            P(("dp", "tensor"), None),
            P(("dp", "tensor")),
        ),
        out_specs=(P(("dp", "tensor"), None), P(("dp", "tensor"), None), P("tensor", "dp")),
        check_vma=False,
    )
```
